512 devices in a mesh: expert: 8 (over x, core), tensor: 64 (over y, z).
Axes of the slice: x: 4, y: 8, z: 8, core: 2. Of those that a mesh axis runs over, the one named last changes fastest.
Arguments:
- tokens: bfloat16 [384, 3072], P('expert', 'tensor'), may hold values from -6 to 6
- cotangent: bfloat16 [384, 3072], P('expert', 'tensor'), may hold values from -6 to 6
- routes: int32 [384, 2], P('expert'), may hold values from 0 to 7, all different within a row; in each aligned block of 48 rows (0 to 47, 48 to 95, ...) at most 20 rows name the same one
- route_weight: float32 [384, 2], P('expert'), may hold values from 0.1 to 1
- w_gate: bfloat16 [8, 3072, 16384], P('expert', None, 'tensor'), may hold values from -0.109375 to 0.109375
- w_up: bfloat16 [8, 3072, 16384], P('expert', None, 'tensor'), may hold values from -0.109375 to 0.109375
- w_down: bfloat16 [8, 16384, 3072], P('expert', 'tensor'), may hold values from -0.125 to 0.125
Outputs:
- mixed: bfloat16 [384, 3072], P('expert', 'tensor')
- input_grad: bfloat16 [384, 3072], P('expert', 'tensor')
The draws below stay inside these ranges and needn't reach their ends.
Inputs may be any that keep to these rules, and one draw needn't show every extreme that they name: `routes`: the two experts of a token differ. Among the 48 tokens of one index of the expert axis, no expert is named by more than 20 of them, and in every draw some expert is named by exactly 20 of them in some such block.
All inputs are finite; a program needn't handle non-finite values.
Results may differ from the reference program's by a relative error of at most 0.0057.
Values may be sent and summed in bfloat16 or wider, within the bound.
A program may use at most 64 MiB of HBM per device.

```python
import math
import jax
import jax.numpy as jnp
import numpy as np
from jax import lax

D = 3072
FF = 16384
TOP = 2
TOK_GRP = 48
EXPERTS = 8
CAP = 20
TOKENS = 384
N_EXPERT = 8


def with_spikes(entries, key, source, target, parts, factor):
    def block_of(dim):
        return (jnp.arange(entries.shape[dim]) // (entries.shape[dim] // parts)).reshape((-1,) + (1,) * (entries.ndim - 1 - dim))

    near = jax.random.permutation(key, parts)[block_of(target)]
    other_side = (block_of(target) + parts // 2) % parts
    return jnp.where((block_of(source) == near) | (block_of(source) == other_side), factor * entries, entries)


def block_scale(key, extent, pieces, least, largest):
    factor_of = 1.0
    for dim, blocks in pieces:
        steps = jax.random.uniform(jax.random.fold_in(jax.random.fold_in(key, 6), dim), (blocks,), jnp.float32, least / len(pieces), largest / len(pieces))
        factor_of = factor_of * jnp.repeat(jnp.exp(steps), extent[dim] // blocks).reshape((-1,) + (1,) * (len(extent) - 1 - dim))
    return factor_of


def routed_block(stream_key, own, number, rows, number_of, top, bound, lean):
    ranking = jax.random.permutation(stream_key, number_of)
    packed, common = shares(number_of, rows * top, bound, lean, True), shares(number_of, rows * top, bound, lean, False)
    places = jnp.arange(number_of)

    def named(tallies, offset_by):
        used = int((tallies > 0).sum())
        fixed = max(1, used // 4)
        moved = fixed + (places - fixed + offset_by * (used - fixed)) % max(1, number_of - fixed)
        return jnp.zeros((number_of,), jnp.int32).at[ranking[jnp.where(places < fixed, places, moved)]].set(jnp.asarray(tallies, jnp.int32))

    tallies = jnp.where(number % 4 == 0, named(packed, number // 4), named(common, number - number // 4 - 1))
    mixed = jax.random.permutation(jax.random.fold_in(own, 3), number_of)
    donor, taker = mixed[0:number_of // 2 * 2:2], mixed[1:number_of // 2 * 2:2]
    room = jnp.minimum(tallies[donor] - 1, bound - tallies[taker]) // 2
    room = jnp.where((donor == ranking[0]) | (taker == ranking[0]) | (tallies[taker] == 0), 0, jnp.maximum(room, 0))
    moved = jax.random.randint(jax.random.fold_in(own, 4), (number_of // 2,), 0, 1 << 20) % (room + 1)
    tallies = tallies.at[donor].add(-moved).at[taker].add(moved)
    items = jnp.searchsorted(jnp.cumsum(tallies), jnp.arange(rows * top), side="right").astype(jnp.int32)
    grid = items.reshape(top, rows).T
    grid = grid[jax.random.permutation(jax.random.fold_in(own, 1), rows)]
    offset_by = jax.random.randint(jax.random.fold_in(own, 2), (rows, 1), 0, top)
    return jnp.take_along_axis(grid, (jnp.arange(top)[None, :] + offset_by) % top, axis=1)


def shares(amount, total, bound, skew, full):
    loads = [(1 << 20) // math.isqrt(standing ** skew) + 1 for standing in range(1, amount + 1)]
    largest = bound if full else min(bound, max(-(-total // amount), total * loads[0] // sum(loads)))
    least = 1 if total - largest >= amount - 1 else 0
    counts, rest = [largest] + [least] * (amount - 1), total - largest - least * (amount - 1)
    while rest > 0:
        movable = [i for i in range(1, amount) if counts[i] < largest] or [i for i in range(1, amount) if counts[i] < bound]
        whole, budget = sum([loads[i] for i in movable]), rest
        for i in movable:
            extra = min(bound - counts[i], max(1, budget * loads[i] // whole), rest)
            counts[i] = counts[i] + extra
            rest = rest - extra
    return np.array(counts)


def centred(rng, extent, width, most, shards=(), held_as=jnp.bfloat16):
    factor_of = block_scale(rng, extent, shards, -0.22, 0.18) if shards else 1.0
    array = jax.random.normal(rng, extent, jnp.float32) * width * factor_of
    return jnp.minimum(jnp.maximum(array, -most), most).astype(held_as)


def bell_draw_with(stream_key, dims, deviation, most, shards, heavy, kind=jnp.bfloat16):
    values = deviation * jax.random.normal(stream_key, dims, jnp.float32)
    if shards:
        values = values * block_scale(stream_key, dims, shards, -0.22, 0.18)
    return jnp.clip(with_spikes(values, jax.random.fold_in(stream_key, 3), *heavy), -most, most).astype(kind)


def setup_inputs(seed: int = 0) -> dict:
    arg_keys = jax.random.split(jax.random.key(seed), 8)
    tokens = centred(arg_keys[0], (TOKENS, D), 1.0, 6.0, ((0, 8), (1, 64)))
    cotangent = centred(arg_keys[1], (TOKENS, D), 1.0, 6.0, ((0, 8), (1, 64)))
    routes_keys = jax.random.split(jax.random.fold_in(arg_keys[2], 1), TOKENS // TOK_GRP)
    routes_turns = jax.random.permutation(jax.random.fold_in(arg_keys[2], 3), TOKENS // TOK_GRP)
    routes = jax.vmap(lambda own, number: routed_block(jax.random.fold_in(arg_keys[2], 2), own, number, TOK_GRP, EXPERTS, TOP, CAP, 2))(routes_keys, routes_turns).reshape((TOKENS, TOP))
    route_weight = jnp.clip(0.1 + 0.9 * jax.random.uniform(arg_keys[3], (TOKENS, TOP), jnp.float32) ** block_scale(arg_keys[3], (TOKENS, TOP), ((0, 8),), -0.2, 0.2), 0.1, 1.0)
    w_gate = centred(arg_keys[4], (EXPERTS, D, FF), D ** -0.5, 0.109375, ((0, 8), (2, 64)))
    w_up = centred(arg_keys[5], (EXPERTS, D, FF), D ** -0.5, 0.109375, ((0, 8), (2, 64)))
    w_down = bell_draw_with(arg_keys[6], (EXPERTS, FF, D), FF ** -0.5, 0.125, ((0, 8), (1, 64)), (1, 2, 64, 4.0))
    return dict(tokens=tokens, cotangent=cotangent, routes=routes, route_weight=route_weight, w_gate=w_gate, w_up=w_up, w_down=w_down)


def swish_parts(gate_pre):
    sigma_gate = jax.nn.sigmoid(gate_pre)
    return sigma_gate, gate_pre * sigma_gate


def reference(tokens, cotangent, routes, route_weight, w_gate, w_up, w_down):
    most_rows = CAP * N_EXPERT
    row_ids = jnp.arange(most_rows, dtype=jnp.int32)

    def per_expert(carry, expert):
        mixed_acc, grad_acc = carry
        chosen = routes == expert
        weight_all = jnp.sum(jnp.where(chosen, route_weight, jnp.zeros_like(route_weight)), axis=1)
        used = jnp.any(chosen, axis=1)
        picked = jnp.nonzero(used, size=most_rows, fill_value=0)[0].astype(jnp.int32)
        valid = row_ids < jnp.sum(used.astype(jnp.int32))
        row_weight = jnp.where(valid, weight_all[picked], jnp.zeros_like(weight_all[picked]))
        token_rows = tokens[picked]
        scaled = (row_weight[:, None] * cotangent[picked].astype(jnp.float32)).astype(jnp.bfloat16)
        gate_mat = w_gate[expert]
        up_mat = w_up[expert]
        down_mat = w_down[expert]
        gate_pre = jnp.dot(token_rows, gate_mat, preferred_element_type=jnp.float32)
        up_pre = jnp.dot(token_rows, up_mat, preferred_element_type=jnp.float32)
        sigma_gate, swish = swish_parts(gate_pre)
        hidden = (swish * up_pre).astype(jnp.bfloat16)
        expert_out = jnp.dot(hidden, down_mat, preferred_element_type=jnp.float32)
        grad_hidden = jnp.dot(scaled, down_mat.T, preferred_element_type=jnp.float32)
        grad_gate = (grad_hidden * up_pre * sigma_gate * (1.0 + gate_pre * (1.0 - sigma_gate))).astype(jnp.bfloat16)
        grad_up = (grad_hidden * swish).astype(jnp.bfloat16)
        grad_rows = jnp.dot(grad_gate, gate_mat.T, preferred_element_type=jnp.float32)
        grad_rows = grad_rows + jnp.dot(grad_up, up_mat.T, preferred_element_type=jnp.float32)
        mixed_acc = mixed_acc.at[picked].add(row_weight[:, None] * expert_out)
        grad_acc = grad_acc.at[picked].add(jnp.where(valid[:, None], grad_rows, jnp.zeros_like(grad_rows)))
        return (mixed_acc, grad_acc), None

    start_zero = jnp.zeros((TOKENS, D), jnp.float32)
    (mixed_acc, grad_acc), _ = lax.scan(per_expert, (start_zero, start_zero), jnp.arange(EXPERTS, dtype=jnp.int32))
    return mixed_acc.astype(jnp.bfloat16), grad_acc.astype(jnp.bfloat16)
```

```python
import functools

import jax
import jax.numpy as jnp
from jax import lax
from jax.experimental import pallas as pl
from jax.experimental.pallas import tpu as pltpu
from jax.sharding import PartitionSpec as P

MESH = pl.DeviceIdType.MESH
BF = jnp.bfloat16
F32 = jnp.float32

GROUPS = 8
SIDE = 8
TOK = 48
CAP = 20
PAD = 32
ROWS = GROUPS * CAP
HALF = ROWS // 2
WIDE = SIDE * TOK
HID = 256
LANES = 128
HIGH = 64
ORDER = (1, 7, 2, 6, 3, 5, 4)


def iota(shape, dim):
    return lax.broadcasted_iota(jnp.int32, shape, dim)


def onehot(cond):
    return jnp.where(cond, 1.0, 0.0).astype(BF)


def mm(a, b):
    return lax.dot_general(a, b, (((1,), (0,)), ((), ())), preferred_element_type=F32)


def mm_tn(a, b):
    return lax.dot_general(a, b, (((0,), (0,)), ((), ())), preferred_element_type=F32)


def mm_nt(a, b):
    return lax.dot_general(a, b, (((1,), (1,)), ((), ())), preferred_element_type=F32)


def kernel(
    tok, cot, routes, rw, wg, wu, wd,
    mixed, gin,
    wgu, wdv, plo, phi, dsend, drecv,
    t1, g1, t2, g2, ms, gs, mr, gr, mp, gp, mq, gq, rsend, rrecv,
    wsem, dss, drs, s1, r1, s2, r2, s3, r3, s4, r4, rss, rrs,
):
    e = lax.axis_index("expert")
    t = lax.axis_index("tensor")
    y = t // SIDE
    z = t % SIDE

    def at_e(d):
        return ((e + d) % GROUPS, t)

    def at_y(d):
        return (e, ((y + d) % SIDE) * SIDE + z)

    def at_z(d):
        return (e, y * SIDE + (z + d) % SIDE)

    loads = []
    for k in range(SIDE):
        loads.append(pltpu.make_async_copy(wg.at[:, k], wgu.at[k, :, :, pl.ds(0, HID)], wsem.at[k]))
        loads.append(pltpu.make_async_copy(wu.at[:, k], wgu.at[k, :, :, pl.ds(HID, HID)], wsem.at[SIDE + k]))
    loads.append(pltpu.make_async_copy(wd, wdv, wsem.at[2 * SIDE]))
    for c in loads:
        c.start()

    bar = pltpu.get_barrier_semaphore()
    for at in (at_e, at_y, at_z):
        for d in range(1, 8):
            pl.semaphore_signal(bar, inc=1, device_id=at(d), device_id_type=MESH)

    def send(src, dst, ss, rs, where):
        c = pltpu.make_async_remote_copy(
            src_ref=src, dst_ref=dst, send_sem=ss, recv_sem=rs, device_id=where, device_id_type=MESH
        )
        c.start()
        return c

    r0, r1_ = routes[:, 0:1], routes[:, 1:2]
    w0, w1 = rw[:, 0:1], rw[:, 1:2]
    lane = iota((TOK, LANES), 1)
    chosen = onehot((lane == r0) | (lane == r1_))
    lower = onehot(iota((TOK, TOK), 1) < iota((TOK, TOK), 0))
    earlier = mm(lower, chosen)
    p0 = jnp.sum(jnp.where(lane == r0, earlier, 0.0), axis=1, keepdims=True).astype(jnp.int32)
    p1 = jnp.sum(jnp.where(lane == r1_, earlier, 0.0), axis=1, keepdims=True).astype(jnp.int32)
    slot = iota((TOK, GROUPS * PAD), 1)
    m0 = onehot(slot == r0 * PAD + p0)
    m1 = onehot(slot == r1_ * PAD + p1)
    emb_lo = onehot(iota((TOK, LANES), 1) == iota((TOK, LANES), 0))
    emb_hi = onehot(iota((TOK, LANES), 1) == iota((TOK, LANES), 0) + HIGH)
    tok_e = mm(tok[...], emb_lo)
    cot_e = mm(cot[...], emb_hi)
    a0 = (tok_e + w0 * cot_e).astype(BF)
    a1 = (tok_e + w1 * cot_e).astype(BF)
    dsend[...] = (mm_tn(m0, a0) + mm_tn(m1, a1)).astype(BF)

    pl.semaphore_wait(bar, 21)

    mine = pl.ds(pl.multiple_of(e * PAD, PAD), PAD)
    copies = []
    for d in range(1, 8):
        there = pl.ds(pl.multiple_of(((e + d) % GROUPS) * PAD, PAD), PAD)
        copies.append(send(dsend.at[there], drecv.at[mine], dss.at[d], drs.at[d], at_e(d)))
    drecv[mine, :] = dsend[mine, :]
    l_ = iota((LANES, WIDE), 0)
    c_ = iota((LANES, WIDE), 1)
    for k in range(SIDE):
        plo[pl.ds(k * LANES, LANES), :] = onehot((c_ - l_ == TOK * k) & (l_ < TOK))
        phi[pl.ds(k * LANES, LANES), :] = onehot((c_ - l_ == TOK * k - HIGH) & (l_ >= HIGH) & (l_ < HIGH + TOK))
    q_ = iota((ROWS, GROUPS * PAD), 1)
    s_ = iota((ROWS, GROUPS * PAD), 0)
    compact = onehot((s_ == (q_ >> 5) * CAP + (q_ & 31)) & ((q_ & 31) < CAP))
    for c in copies:
        c.wait()

    rows = mm(compact, drecv[...])
    lo, hi = rows[:HALF], rows[HALF:]
    low_lane = iota((HALF, LANES), 1) < HIGH
    t1[y] = jnp.where(low_lane, lo, pltpu.roll(hi, HIGH, 1)).astype(BF)
    g1[z] = jnp.where(low_lane, pltpu.roll(lo, HIGH, 1), hi).astype(BF)

    copies = []
    for d in range(1, 8):
        copies.append(send(t1.at[y], t1.at[y], s1.at[0, d], r1.at[0, d], at_y(d)))
        copies.append(send(g1.at[z], g1.at[z], s1.at[1, d], r1.at[1, d], at_z(d)))
    for c in copies:
        c.wait()

    def unpack(ref):
        flat = jnp.concatenate([ref[k] for k in range(SIDE)], axis=1)
        return jnp.concatenate([mm(flat, plo[...]), mm(flat, phi[...])], axis=0).astype(BF)

    t2[0] = unpack(t1)
    g2[0] = unpack(g1)

    sends = {}
    for d in ORDER:
        sends[d] = (
            send(t2.at[0], t2.at[d], s2.at[0, d], r2.at[0, d], at_z(d)),
            send(g2.at[0], g2.at[d], s2.at[1, d], r2.at[1, d], at_y(d)),
        )
    for c in loads:
        c.wait()

    def wcols(k):
        return pl.ds(pl.multiple_of(k * WIDE, LANES), WIDE)

    def wrows(k):
        return wgu[k].reshape(WIDE, 2 * HID)

    gate_up = mm(t2[0], wrows(z))
    grad_h = mm_nt(g2[0], wdv[:, wcols(y)])
    for d in ORDER:
        sends[d][0].wait()
        gate_up += mm(t2[d], wrows((z + SIDE - d) % SIDE))
        sends[d][1].wait()
        grad_h += mm_nt(g2[d], wdv[:, wcols((y + SIDE - d) % SIDE)])

    gate, up = gate_up[:, :HID], gate_up[:, HID:]
    sig = 1.0 / (1.0 + jnp.exp(-gate))
    swish = gate * sig
    hidden = (swish * up).astype(BF)
    grad_gate = (grad_h * up * sig * (1.0 + gate * (1.0 - sig))).astype(BF)
    grad_up = (grad_h * swish).astype(BF)
    grads = jnp.concatenate([grad_gate, grad_up], axis=1)

    sends = {}
    for d in ORDER:
        ms[d] = mm(hidden, wdv[:, wcols((y + d) % SIDE)]).astype(BF)
        gs[d] = mm_nt(grads, wrows((z + d) % SIDE)).astype(BF)
        sends[d] = (
            send(ms.at[d], mr.at[d], s3.at[0, d], r3.at[0, d], at_y(d)),
            send(gs.at[d], gr.at[d], s3.at[1, d], r3.at[1, d], at_z(d)),
        )
    msum = mm(hidden, wdv[:, wcols(y)])
    gsum = mm_nt(grads, wrows(z))
    for d in ORDER:
        sends[d][0].wait()
        msum += mr[d].astype(F32)
        sends[d][1].wait()
        gsum += gr[d].astype(F32)

    def pack(total):
        r = total.astype(BF)
        return mm_nt(r[:HALF], plo[...]) + mm_nt(r[HALF:], phi[...])

    mall = pack(msum).astype(BF)
    gall = pack(gsum).astype(BF)
    for k in range(SIDE):
        mp[k] = mall[:, k * LANES:(k + 1) * LANES]
        gp[k] = gall[:, k * LANES:(k + 1) * LANES]
    copies = []
    for d in range(1, 8):
        copies.append(send(mp.at[(z + d) % SIDE], mq.at[d], s4.at[0, d], r4.at[0, d], at_z(d)))
        copies.append(send(gp.at[(y + d) % SIDE], gq.at[d], s4.at[1, d], r4.at[1, d], at_y(d)))
    mtot = mp[z].astype(F32)
    gtot = gp[y].astype(F32)
    for c in copies:
        c.wait()
    for d in range(1, 8):
        mtot += mq[d].astype(F32)
        gtot += gq[d].astype(F32)

    lo = jnp.where(low_lane, mtot, pltpu.roll(gtot, HIGH, 1))
    hi = jnp.where(low_lane, pltpu.roll(mtot, HIGH, 1), gtot)
    both = jnp.concatenate([lo, hi], axis=0).astype(BF)
    rsend[...] = mm_tn(compact, both).astype(BF)
    copies = []
    for d in range(1, 8):
        there = pl.ds(pl.multiple_of(((e + d) % GROUPS) * PAD, PAD), PAD)
        copies.append(send(rsend.at[there], rrecv.at[mine], rss.at[d], rrs.at[d], at_e(d)))
    rrecv[mine, :] = rsend[mine, :]
    for c in copies:
        c.wait()
    back = rrecv[...]
    b0 = mm(m0, back)
    b1 = mm(m1, back)
    mixed[...] = (w0 * b0 + w1 * b1)[:, :TOK].astype(BF)
    gin[...] = pltpu.roll(b0 + b1, HIGH, 1)[:, :TOK].astype(BF)


def shards(tokens, cotangent, routes, route_weight, w_gate, w_up, w_down):
    vm = pl.BlockSpec(memory_space=pltpu.VMEM)
    hbm = pl.BlockSpec(memory_space=pl.ANY)
    dma = pltpu.SemaphoreType.DMA
    small = pltpu.VMEM((SIDE, HALF, LANES), BF)
    big = pltpu.VMEM((SIDE, ROWS, WIDE), BF)
    table = pltpu.VMEM((SIDE * LANES, WIDE), BF)
    block = pltpu.VMEM((GROUPS * PAD, LANES), BF)
    out = jax.ShapeDtypeStruct((TOK, TOK), BF)
    return pl.pallas_call(
        kernel,
        out_shape=(out, out),
        in_specs=[vm] * 4 + [hbm] * 3,
        out_specs=(vm, vm),
        scratch_shapes=[
            pltpu.VMEM((SIDE, SIDE, TOK, 2 * HID), BF),
            pltpu.VMEM((HID, SIDE * WIDE), BF),
            table, table, block, block,
            small, small, big, big, big, big, big, big, small, small, small, small, block, block,
            dma((2 * SIDE + 1,)), dma((8,)), dma((8,)),
            dma((2, 8)), dma((2, 8)), dma((2, 8)), dma((2, 8)),
            dma((2, 8)), dma((2, 8)), dma((2, 8)), dma((2, 8)),
            dma((8,)), dma((8,)),
        ],
        compiler_params=pltpu.CompilerParams(
            collective_id=0, has_side_effects=True, vmem_limit_bytes=40 * 2**20
        ),
        name="moe",
    )(
        tokens, cotangent, routes, route_weight,
        w_gate.reshape(SIDE, SIDE, TOK, HID), w_up.reshape(SIDE, SIDE, TOK, HID), w_down[0],
    )


def solution(mesh):
    return jax.shard_map(
        shards,
        mesh=mesh,
        in_specs=(
            P("expert", "tensor"),
            P("expert", "tensor"),
            P("expert", None),
            P("expert", None),
            P("expert", None, "tensor"),
            P("expert", None, "tensor"),
            P("expert", "tensor", None),
        ),
        out_specs=(P("expert", "tensor"), P("expert", "tensor")),
        check_vma=False,
    )
```

```python
import functools

import jax
import jax.numpy as jnp
from jax import lax
from jax.experimental import pallas as pl
from jax.experimental.pallas import tpu as pltpu
from jax.sharding import PartitionSpec as P

MESH = pl.DeviceIdType.MESH
BF = jnp.bfloat16
F32 = jnp.float32

GROUPS = 8
SIDE = 8
TOK = 48
CAP = 20
PAD = 32
ROWS = GROUPS * CAP
HALF = ROWS // 2
WIDE = SIDE * TOK
HID = 256
LANES = 128
HIGH = 64


def iota(shape, dim):
    return lax.broadcasted_iota(jnp.int32, shape, dim)


def onehot(cond):
    return jnp.where(cond, 1.0, 0.0).astype(BF)


def mm(a, b):
    return lax.dot_general(a, b, (((1,), (0,)), ((), ())), preferred_element_type=F32)


def mm_tn(a, b):
    return lax.dot_general(a, b, (((0,), (0,)), ((), ())), preferred_element_type=F32)


def mm_nt(a, b):
    return lax.dot_general(a, b, (((1,), (1,)), ((), ())), preferred_element_type=F32)


def kernel(
    tok_h, cot_h, routes_h, rw_h, wg, wu, wd,
    mixed, gin,
    tok, cot, routes, rw, isem,
    wgu, wdv, plo, phi, dsend, drecv,
    t1, g1, t2, g2, pm, pg, ms, gs, mr, gr, mp, gp, mq, gq, rsend, rrecv,
    wsem, dss, drs, s1, r1, s2, r2, s3, r3, s4, r4, rss, rrs,
):
    e = lax.axis_index("expert")
    t = lax.axis_index("tensor")
    y = t // SIDE
    z = t % SIDE

    def at_e(d):
        return ((e + d) % GROUPS, t)

    def at_y(d):
        return (e, ((y + d) % SIDE) * SIDE + z)

    def at_z(d):
        return (e, y * SIDE + (z + d) % SIDE)

    first = [
        pltpu.make_async_copy(a, b, isem.at[k])
        for k, (a, b) in enumerate(((routes_h, routes), (tok_h, tok), (cot_h, cot), (rw_h, rw)))
    ]
    for c in first:
        c.start()
    loads = []
    for k in range(SIDE):
        loads.append(pltpu.make_async_copy(wg.at[:, k], wgu.at[k, :, :, pl.ds(0, HID)], wsem.at[k]))
        loads.append(pltpu.make_async_copy(wu.at[:, k], wgu.at[k, :, :, pl.ds(HID, HID)], wsem.at[SIDE + k]))
    loads.append(pltpu.make_async_copy(wd, wdv, wsem.at[2 * SIDE]))
    for c in loads:
        c.start()

    bar = pltpu.get_barrier_semaphore()
    for at in (at_e, at_y, at_z):
        for d in range(1, 8):
            pl.semaphore_signal(bar, inc=1, device_id=at(d), device_id_type=MESH)

    def send(src, dst, ss, rs, where):
        c = pltpu.make_async_remote_copy(
            src_ref=src, dst_ref=dst, send_sem=ss, recv_sem=rs, device_id=where, device_id_type=MESH
        )
        c.start()
        return c

    for c in first:
        c.wait()
    eye = iota((TOK, TOK), 0) == iota((TOK, TOK), 1)

    def column(row):
        return jnp.sum(jnp.where(eye, row, 0.0), axis=1, keepdims=True)

    ids = routes[...].astype(F32)
    r0, r1_ = column(ids[0:1]).astype(jnp.int32), column(ids[1:2]).astype(jnp.int32)
    w0, w1 = column(rw[0:1, :]), column(rw[1:2, :])
    lane = iota((TOK, LANES), 1)
    chosen = onehot((lane == r0) | (lane == r1_))
    lower = onehot(iota((TOK, TOK), 1) < iota((TOK, TOK), 0))
    earlier = mm(lower, chosen)
    p0 = jnp.sum(jnp.where(lane == r0, earlier, 0.0), axis=1, keepdims=True).astype(jnp.int32)
    p1 = jnp.sum(jnp.where(lane == r1_, earlier, 0.0), axis=1, keepdims=True).astype(jnp.int32)
    slot = iota((TOK, GROUPS * PAD), 1)
    m0 = onehot(slot == r0 * PAD + p0)
    m1 = onehot(slot == r1_ * PAD + p1)
    emb_lo = onehot(iota((TOK, LANES), 1) == iota((TOK, LANES), 0))
    emb_hi = onehot(iota((TOK, LANES), 1) == iota((TOK, LANES), 0) + HIGH)
    tok_e = mm(tok[...], emb_lo)
    cot_e = mm(cot[...], emb_hi)
    a0 = (tok_e + w0 * cot_e).astype(BF)
    a1 = (tok_e + w1 * cot_e).astype(BF)
    dsend[...] = (mm_tn(m0, a0) + mm_tn(m1, a1)).astype(BF)

    pl.semaphore_wait(bar, 21)

    mine = pl.ds(pl.multiple_of(e * PAD, PAD), PAD)
    copies = []
    for d in range(1, 8):
        there = pl.ds(pl.multiple_of(((e + d) % GROUPS) * PAD, PAD), PAD)
        copies.append(send(dsend.at[there], drecv.at[mine], dss.at[d], drs.at[d], at_e(d)))
    drecv[mine, :] = dsend[mine, :]
    l_ = iota((LANES, WIDE), 0)
    c_ = iota((LANES, WIDE), 1)
    for k in range(SIDE):
        plo[pl.ds(k * LANES, LANES), :] = onehot((c_ - l_ == TOK * k) & (l_ < TOK))
        phi[pl.ds(k * LANES, LANES), :] = onehot((c_ - l_ == TOK * k - HIGH) & (l_ >= HIGH) & (l_ < HIGH + TOK))
    q_ = iota((ROWS, GROUPS * PAD), 1)
    s_ = iota((ROWS, GROUPS * PAD), 0)
    compact = onehot((s_ == (q_ >> 5) * CAP + (q_ & 31)) & ((q_ & 31) < CAP))
    for c in copies:
        c.wait()

    rows = mm(compact, drecv[...])
    lo, hi = rows[:HALF], rows[HALF:]
    low_lane = iota((HALF, LANES), 1) < HIGH
    t1[y] = jnp.where(low_lane, lo, pltpu.roll(hi, HIGH, 1)).astype(BF)
    g1[z] = jnp.where(low_lane, pltpu.roll(lo, HIGH, 1), hi).astype(BF)

    copies = []
    for d in range(1, 8):
        copies.append(send(t1.at[y], t1.at[y], s1.at[0, d], r1.at[0, d], at_y(d)))
        copies.append(send(g1.at[z], g1.at[z], s1.at[1, d], r1.at[1, d], at_z(d)))
    for c in copies:
        c.wait()

    def unpack(ref):
        flat = jnp.concatenate([ref[k] for k in range(SIDE)], axis=1)
        return jnp.concatenate([mm(flat, plo[...]), mm(flat, phi[...])], axis=0).astype(BF)

    t2[0] = unpack(t1)
    g2[0] = unpack(g1)

    up_ring = ((1, 0), (1, 1), (2, 0), (2, 1), (3, 0), (3, 1), (4, 0))
    down_ring = ((7, 1), (7, 0), (6, 1), (6, 0), (5, 1), (5, 0), (4, 1))

    def half(h):
        return pl.ds(h * HALF, HALF)

    def hop(buf, way, n, at, a):
        k, h = (up_ring, down_ring)[way][n]
        before = (k - 1) if way == 0 else (k + 1) % SIDE
        return send(
            buf.at[before, half(h)], buf.at[k, half(h)],
            s2.at[a, way, n], r2.at[a, way, n], at(1 if way == 0 else SIDE - 1),
        )

    streams = [(t2, 0, at_z, 0), (t2, 1, at_z, 0), (g2, 0, at_y, 1), (g2, 1, at_y, 1)]
    hops = [[hop(buf, way, n, at, a) for n in range(2)] for buf, way, at, a in streams]
    for c in loads:
        c.wait()

    def wcols(k):
        return pl.ds(pl.multiple_of(k * WIDE, LANES), WIDE)

    def wrows(k):
        return wgu[k].reshape(WIDE, 2 * HID)

    gate_up = mm(t2[0], wrows(z))
    grad_h = mm_nt(g2[0], wdv[:, wcols(y)])
    for n in range(7):
        for c, (buf, way, at, a) in zip(hops, streams):
            c[n].wait_recv()
            if n + 2 < 7:
                c.append(hop(buf, way, n + 2, at, a))
        if n % 2 == 1 or n == 6:
            k = n // 2 + 1
            for d in (k, SIDE - k) if k < 4 else (4,):
                gate_up += mm(t2[d], wrows((z + SIDE - d) % SIDE))
                grad_h += mm_nt(g2[d], wdv[:, wcols((y + SIDE - d) % SIDE)])
    for c in hops:
        for x in c:
            x.wait_send()

    gate, up = gate_up[:, :HID], gate_up[:, HID:]
    sig = 1.0 / (1.0 + jnp.exp(-gate))
    swish = gate * sig
    hidden = (swish * up).astype(BF)
    grad_gate = (grad_h * up * sig * (1.0 + gate * (1.0 - sig))).astype(BF)
    grad_up = (grad_h * swish).astype(BF)
    grads = jnp.concatenate([grad_gate, grad_up], axis=1)

    up_sum = ((4, 0), (3, 1), (3, 0), (2, 1), (2, 0), (1, 1), (1, 0))
    down_sum = ((4, 1), (5, 0), (5, 1), (6, 0), (6, 1), (7, 0), (7, 1))

    def partial(d):
        pm[d] = mm(hidden, wdv[:, wcols((y + d) % SIDE)])
        pg[d] = mm_nt(grads, wrows((z + d) % SIDE))

    streams = [(pm, ms, mr, 0, at_y, 0), (pm, ms, mr, 1, at_y, 0), (pg, gs, gr, 0, at_z, 1), (pg, gs, gr, 1, at_z, 1)]
    hops = [[] for _ in streams]

    def pass_on(n):
        for c, (part, sbuf, rbuf, way, at, a) in zip(hops, streams):
            d, h = (up_sum, down_sum)[way][n]
            value = part[d, half(h), :]
            if n >= 2:
                c[n - 2].wait_recv()
                value += rbuf[way, n - 2].astype(F32)
            sbuf[way, n] = value.astype(BF)
            c.append(send(
                sbuf.at[way, n], rbuf.at[way, n],
                s3.at[a, way, n], r3.at[a, way, n], at(1 if way == 0 else SIDE - 1),
            ))

    partial(4)
    pass_on(0)
    partial(3)
    partial(5)
    pass_on(1)
    partial(2)
    partial(6)
    pass_on(2)
    pass_on(3)
    partial(1)
    partial(7)
    pass_on(4)
    pass_on(5)
    partial(0)
    pass_on(6)
    sums = []
    for i, (part, rbuf) in enumerate(((pm, mr), (pg, gr))):
        one, two = hops[2 * i], hops[2 * i + 1]
        halves = [None, None]
        for n in (5, 6):
            one[n].wait_recv()
            two[n].wait_recv()
        halves[0] = part[0, half(0), :] + rbuf[0, 6].astype(F32) + rbuf[1, 5].astype(F32)
        halves[1] = part[0, half(1), :] + rbuf[0, 5].astype(F32) + rbuf[1, 6].astype(F32)
        sums.append(jnp.concatenate(halves, axis=0))
    msum, gsum = sums
    for c in hops:
        for x in c:
            x.wait_send()

    def pack(total):
        r = total.astype(BF)
        return mm_nt(r[:HALF], plo[...]) + mm_nt(r[HALF:], phi[...])

    mall = pack(msum).astype(BF)
    gall = pack(gsum).astype(BF)
    for k in range(SIDE):
        mp[k] = mall[:, k * LANES:(k + 1) * LANES]
        gp[k] = gall[:, k * LANES:(k + 1) * LANES]
    copies = []
    for d in range(1, 8):
        copies.append(send(mp.at[(z + d) % SIDE], mq.at[d], s4.at[0, d], r4.at[0, d], at_z(d)))
        copies.append(send(gp.at[(y + d) % SIDE], gq.at[d], s4.at[1, d], r4.at[1, d], at_y(d)))
    mtot = mp[z].astype(F32)
    gtot = gp[y].astype(F32)
    for c in copies:
        c.wait()
    for d in range(1, 8):
        mtot += mq[d].astype(F32)
        gtot += gq[d].astype(F32)

    lo = jnp.where(low_lane, mtot, pltpu.roll(gtot, HIGH, 1))
    hi = jnp.where(low_lane, pltpu.roll(mtot, HIGH, 1), gtot)
    both = jnp.concatenate([lo, hi], axis=0).astype(BF)
    rsend[...] = mm_tn(compact, both).astype(BF)
    copies = []
    for d in range(1, 8):
        there = pl.ds(pl.multiple_of(((e + d) % GROUPS) * PAD, PAD), PAD)
        copies.append(send(rsend.at[there], rrecv.at[mine], rss.at[d], rrs.at[d], at_e(d)))
    rrecv[mine, :] = rsend[mine, :]
    for c in copies:
        c.wait()
    back = rrecv[...]
    b0 = mm(m0, back)
    b1 = mm(m1, back)
    mixed[...] = (w0 * b0 + w1 * b1)[:, :TOK].astype(BF)
    gin[...] = pltpu.roll(b0 + b1, HIGH, 1)[:, :TOK].astype(BF)


def shards(tokens, cotangent, routes, route_weight, w_gate, w_up, w_down):
    vm = pl.BlockSpec(memory_space=pltpu.VMEM)
    hbm = pl.BlockSpec(memory_space=pl.ANY)
    dma = pltpu.SemaphoreType.DMA
    small = pltpu.VMEM((SIDE, HALF, LANES), BF)
    big = pltpu.VMEM((SIDE, ROWS, WIDE), BF)
    table = pltpu.VMEM((SIDE * LANES, WIDE), BF)
    block = pltpu.VMEM((GROUPS * PAD, LANES), BF)
    tall = pltpu.VMEM((SIDE, ROWS, WIDE), F32)
    sums = pltpu.VMEM((2, 7, HALF, WIDE), BF)
    out = jax.ShapeDtypeStruct((TOK, TOK), BF)
    return pl.pallas_call(
        kernel,
        out_shape=(out, out),
        in_specs=[hbm] * 7,
        out_specs=(vm, vm),
        scratch_shapes=[
            pltpu.VMEM((TOK, TOK), BF), pltpu.VMEM((TOK, TOK), BF),
            pltpu.VMEM((2, TOK), jnp.int32), pltpu.VMEM((2, TOK), F32), dma((4,)),
            pltpu.VMEM((SIDE, SIDE, TOK, 2 * HID), BF),
            pltpu.VMEM((HID, SIDE * WIDE), BF),
            table, table, block, block,
            small, small, big, big, tall, tall, sums, sums, sums, sums, small, small, small, small, block, block,
            dma((2 * SIDE + 1,)), dma((8,)), dma((8,)),
            dma((2, 8)), dma((2, 8)), dma((2, 2, 7)), dma((2, 2, 7)),
            dma((2, 2, 7)), dma((2, 2, 7)), dma((2, 8)), dma((2, 8)),
            dma((8,)), dma((8,)),
        ],
        compiler_params=pltpu.CompilerParams(
            collective_id=0, has_side_effects=True, vmem_limit_bytes=60 * 2**20
        ),
        name="moe",
    )(
        tokens, cotangent, routes.T, route_weight.T,
        w_gate.reshape(SIDE, SIDE, TOK, HID), w_up.reshape(SIDE, SIDE, TOK, HID), w_down[0],
    )


def solution(mesh):
    return jax.shard_map(
        shards,
        mesh=mesh,
        in_specs=(
            P("expert", "tensor"),
            P("expert", "tensor"),
            P("expert", None),
            P("expert", None),
            P("expert", None, "tensor"),
            P("expert", None, "tensor"),
            P("expert", "tensor", None),
        ),
        out_specs=(P("expert", "tensor"), P("expert", "tensor")),
        check_vma=False,
    )
```

```python
import jax
import jax.numpy as jnp
from jax import lax
from jax.experimental import pallas as pl
from jax.experimental.pallas import tpu as pltpu
from jax.sharding import PartitionSpec as P

MESH = pl.DeviceIdType.MESH
BF = jnp.bfloat16
F32 = jnp.float32

GROUPS = 8
SIDE = 8
TOK = 48
CAP = 20
PAD = 48
ROWS = GROUPS * CAP
HALF = ROWS // 2
WIDE = SIDE * TOK
HID = 256
LANES = 128
FAR = (4, 3, 5, 2, 6, 1, 7)
NEAR = (0, 1, 7, 2, 6, 3, 5, 4)


def iota(shape, dim):
    return lax.broadcasted_iota(jnp.int32, shape, dim)


def onehot(cond):
    return jnp.where(cond, 1.0, 0.0).astype(BF)


def mm(a, b):
    return lax.dot_general(a, b, (((1,), (0,)), ((), ())), preferred_element_type=F32)


def mm_tn(a, b):
    return lax.dot_general(a, b, (((0,), (0,)), ((), ())), preferred_element_type=F32)


def mm_nt(a, b):
    return lax.dot_general(a, b, (((1,), (1,)), ((), ())), preferred_element_type=F32)


def half(h):
    return pl.ds(h * HALF, HALF)


def kernel(
    tok_h, cot_h, routes_h, rw_h, wg, wu, wd,
    mixed, gin,
    tok, cot, routes, rw, isem,
    wgu, wdv, spread, comp, dsend, drecv, rsend, rrecv,
    t1, g1, t2, g2, pm, pg, ms, gs, mr, gr, mp, gp, mq, gq,
    wsem, s1, r1, ds_, dr, s2, r2, s3, r3, rs_, rr, s4, r4,
):
    e = lax.axis_index("expert")
    t = lax.axis_index("tensor")
    y = t // SIDE
    z = t % SIDE

    def at_e(d):
        return ((e + d + GROUPS) % GROUPS, t)

    def at_y(d):
        return (e, ((y + d + SIDE) % SIDE) * SIDE + z)

    def at_z(d):
        return (e, y * SIDE + (z + d + SIDE) % SIDE)

    def send(src, dst, ss, rs, where):
        c = pltpu.make_async_remote_copy(
            src_ref=src, dst_ref=dst, send_sem=ss, recv_sem=rs, device_id=where, device_id_type=MESH
        )
        c.start()
        return c

    first = [
        pltpu.make_async_copy(a, b, isem.at[k])
        for k, (a, b) in enumerate(((tok_h, tok), (cot_h, cot), (routes_h, routes), (rw_h, rw)))
    ]
    for c in first:
        c.start()
    bar = pltpu.get_barrier_semaphore()
    for at in (at_y, at_z, at_e):
        for d in FAR:
            pl.semaphore_signal(bar, inc=1, device_id=at(d), device_id_type=MESH)
    loads = []
    for k in range(SIDE):
        loads.append(pltpu.make_async_copy(wg.at[:, k], wgu.at[k, :, :, pl.ds(0, HID)], wsem.at[k]))
        loads.append(pltpu.make_async_copy(wu.at[:, k], wgu.at[k, :, :, pl.ds(HID, HID)], wsem.at[SIDE + k]))
    loads.append(pltpu.make_async_copy(wd, wdv, wsem.at[2 * SIDE]))

    zero = jnp.zeros((TOK, LANES), BF)
    t1[y] = zero
    g1[z] = zero
    first[0].wait()
    first[1].wait()
    t1[y, :, :TOK] = tok[...]
    g1[z, :, :TOK] = cot[...]
    pl.semaphore_wait(bar, 21)

    copies = []
    for d in FAR:
        copies.append(send(t1.at[y], t1.at[y], s1.at[0, d], r1.at[0, d], at_y(d)))
        copies.append(send(g1.at[z], g1.at[z], s1.at[1, d], r1.at[1, d], at_z(d)))
    for c in loads:
        c.start()

    first[2].wait()
    first[3].wait()
    eye = iota((TOK, TOK), 0) == iota((TOK, TOK), 1)

    def column(row):
        return jnp.sum(jnp.where(eye, row, 0.0), axis=1, keepdims=True)

    ids = routes[...].astype(F32)
    e0, e1 = column(ids[0:1]).astype(jnp.int32), column(ids[1:2]).astype(jnp.int32)
    w0, w1 = column(rw[0:1, :]), column(rw[1:2, :])
    lane = iota((TOK, LANES), 1)
    chosen = onehot((lane == e0) | (lane == e1))
    lower = onehot(iota((TOK, TOK), 1) < iota((TOK, TOK), 0))
    earlier = mm(lower, chosen)
    p0 = jnp.sum(jnp.where(lane == e0, earlier, 0.0), axis=1, keepdims=True).astype(jnp.int32) + e0 * PAD
    p1 = jnp.sum(jnp.where(lane == e1, earlier, 0.0), axis=1, keepdims=True).astype(jnp.int32) + e1 * PAD
    slot = iota((TOK, GROUPS * PAD), 1)
    m0 = onehot(slot == p0)
    m1 = onehot(slot == p1)
    n0 = onehot(slot == p0 + CAP)
    n1 = onehot(slot == p1 + CAP)
    l_ = iota((LANES, WIDE), 0)
    c_ = iota((LANES, WIDE), 1)
    for k in range(SIDE):
        spread[pl.ds(k * LANES, LANES), :] = onehot((c_ - l_ == TOK * k) & (l_ < TOK))
    q_ = iota((HALF, GROUPS // 2 * PAD), 1)
    s_ = iota((HALF, GROUPS // 2 * PAD), 0)
    group = ((q_.astype(F32) + 0.5) * (1.0 / PAD)).astype(jnp.int32)
    place = q_ - group * PAD
    row = group * CAP + place
    comp[pl.ds(0, HALF), :] = onehot((row == s_) & (place < CAP))
    comp[pl.ds(HALF, HALF), :] = onehot((row == s_ + CAP) & (place >= CAP) & (place < 2 * CAP))
    for c in copies:
        c.wait()

    def unpack(ref):
        return mm(jnp.concatenate([ref[k] for k in range(SIDE)], axis=1), spread[...])

    tu = unpack(t1).astype(BF)
    gu = unpack(g1)
    left = jnp.concatenate([m0 + m1, n0, n1], axis=0)
    right = jnp.concatenate([tu, (w0 * gu).astype(BF), (w1 * gu).astype(BF)], axis=0)
    dsend[...] = mm_tn(left, right).astype(BF)
    mine = pl.ds(pl.multiple_of(e * PAD, PAD), PAD)

    def there(d):
        return pl.ds(pl.multiple_of(((e + d) % GROUPS) * PAD, PAD), PAD)

    def place_of(d):
        return pl.ds(NEAR.index(d) * PAD, PAD)

    copies = {}
    for o in NEAR[1:]:
        d = GROUPS - o
        copies[o] = send(dsend.at[there(d)], drecv.at[place_of(o)], ds_.at[d], dr.at[d], at_e(d))
    drecv[place_of(0), :] = dsend[mine, :]

    def arrive(b):
        for o in NEAR[4 * b : 4 * b + 4]:
            if o:
                copies[o].wait_recv()
        rows = mm(comp[...], drecv[pl.ds(b * 4 * PAD, 4 * PAD), :]).astype(BF)
        t2[0, half(b), :] = rows[:HALF]
        g2[0, half(b), :] = rows[HALF:]

    pairs = ((t2, at_z, 0), (g2, at_y, 1))
    moves = {}

    def go(b, n, src, dst, dist):
        for buf, at, a in pairs:
            moves[a, b, n] = send(
                buf.at[src, half(b)], buf.at[dst, half(b)], s2.at[a, b, n], r2.at[a, b, n], at(dist)
            )

    def arrived(b, *ns):
        for n in ns:
            for a in range(2):
                moves[a, b, n].wait_recv()

    def wcols(k):
        return pl.ds(pl.multiple_of(k * WIDE, LANES), WIDE)

    def wrows(k):
        return wgu[k].reshape(WIDE, 2 * HID)

    acc = [[0.0, 0.0], [0.0, 0.0]]

    def use(b, *ds):
        for d in ds:
            acc[b][0] += mm(t2[d, half(b), :], wrows((z + SIDE - d) % SIDE))
            acc[b][1] += mm_nt(g2[d, half(b), :], wdv[:, wcols((y + SIDE - d) % SIDE)])

    def two(b):
        go(b, 0, 0, 2, 2)
        go(b, 1, 0, 6, -2)

    def one(b):
        go(b, 2, 0, 1, 1)
        go(b, 3, 0, 7, -1)

    def pass_on(b):
        for n in (b, 1 - b):
            arrived(b, n)
            src, step = (2, 1) if n == 0 else (6, -1)
            if n == b:
                go(b, 6, src, 4, 2 * step)
            go(b, 4 + n, src, src + step, step)

    state = [None, None]

    def activate(b):
        gate, up = acc[b][0][:, :HID], acc[b][0][:, HID:]
        grad_h = acc[b][1]
        sig = 1.0 / (1.0 + jnp.exp(-gate))
        swish = gate * sig
        hidden = (swish * up).astype(BF)
        grad_gate = (grad_h * up * sig * (1.0 + gate * (1.0 - sig))).astype(BF)
        grad_up = (grad_h * swish).astype(BF)
        state[b] = (hidden, jnp.concatenate([grad_gate, grad_up], axis=1))

    sums = ((ms, mr, at_y, 0), (gs, gr, at_z, 1))
    hops = {}

    def term(b, d):
        hidden, grads = state[b]
        return mm(hidden, wdv[:, wcols((y + d) % SIDE)]), mm_nt(grads, wrows((z + d) % SIDE))

    def give(b, n, values, dist):
        for (sbuf, rbuf, at, a), value in zip(sums, values):
            sbuf[b, n] = value.astype(BF)
            hops[a, b, n] = send(sbuf.at[b, n], rbuf.at[b, n], s3.at[a, b, n], r3.at[a, b, n], at(dist))

    def taken(b, n):
        values = []
        for _, rbuf, _, a in sums:
            hops[a, b, n].wait_recv()
            values.append(rbuf[b, n].astype(F32))
        return values

    def add(*terms):
        return [sum(vs[1:], vs[0]) for vs in zip(*terms)]

    def start_sums(b):
        give(b, 0, term(b, 4), 2 if b == 0 else -2)
        give(b, 1, term(b, 3), 1)
        give(b, 2, term(b, 5), -1)
        give(b, 3, term(b, 1), 1)
        give(b, 4, term(b, 7), -1)
        for i, d in enumerate((2, 6)):
            pm[b, i], pg[b, i] = term(b, d)

    def kept(b, d):
        return [pm[b, (d - 2) // 4], pg[b, (d - 2) // 4]]

    def middle_sums(b):
        for way in (1 - b, b):
            d, n = ((2, 1), (6, 2))[way]
            parts = [kept(b, d), taken(b, n)]
            if way == b:
                parts.append(taken(b, 0))
            give(b, 5 + way, add(*parts), 2 if way == 0 else -2)

    backs = []

    def end_sums(b):
        total = add(term(b, 0), taken(b, 3), taken(b, 4), taken(b, 5), taken(b, 6))
        both = jnp.concatenate([v.astype(BF) for v in total], axis=0)
        rsend[pl.ds(b * 4 * PAD, 4 * PAD), :] = mm_tn(comp[...], both).astype(BF)
        for o in NEAR[4 * b : 4 * b + 4]:
            if o:
                backs.append(send(rsend.at[place_of(o)], rrecv.at[mine], rs_.at[o], rr.at[o], at_e(o)))
            else:
                rrecv[mine, :] = rsend[place_of(0), :]

    arrive(0)
    two(0)
    one(0)
    arrive(1)
    two(1)
    for c in loads:
        c.wait()
    use(0, 0)
    pass_on(0)
    one(1)
    use(0, 2, 6)
    arrived(0, 2, 3)
    use(0, 1, 7)
    pass_on(1)
    arrived(0, 4, 5, 6)
    use(0, 3, 5, 4)
    activate(0)
    start_sums(0)
    use(1, 0, 2, 6)
    arrived(1, 2, 3)
    use(1, 1, 7)
    middle_sums(0)
    arrived(1, 4, 5, 6)
    use(1, 3, 5, 4)
    activate(1)
    start_sums(1)
    end_sums(0)
    middle_sums(1)
    end_sums(1)
    for c in backs:
        c.wait()
    back = rrecv[...]
    out = (w0 * mm(m0, back) + w1 * mm(m1, back)).astype(BF)
    grad = mm(n0 + n1, back).astype(BF)

    mall = mm_nt(out, spread[...]).astype(BF)
    gall = mm_nt(grad, spread[...]).astype(BF)
    for k in range(SIDE):
        mp[k] = mall[:, k * LANES:(k + 1) * LANES]
        gp[k] = gall[:, k * LANES:(k + 1) * LANES]
    last = []
    for d in FAR:
        last.append(send(mp.at[(z + d) % SIDE], mq.at[d], s4.at[0, d], r4.at[0, d], at_z(d)))
        last.append(send(gp.at[(y + d) % SIDE], gq.at[d], s4.at[1, d], r4.at[1, d], at_y(d)))
    mtot = mp[z].astype(F32)
    gtot = gp[y].astype(F32)
    for c in last:
        c.wait()
    for d in range(1, 8):
        mtot += mq[d].astype(F32)
        gtot += gq[d].astype(F32)
    mixed[...] = mtot[:, :TOK].astype(BF)
    gin[...] = gtot[:, :TOK].astype(BF)

    for c in (*copies.values(), *moves.values(), *hops.values()):
        c.wait_send()


def shards(tokens, cotangent, routes, route_weight, w_gate, w_up, w_down):
    vm = pl.BlockSpec(memory_space=pltpu.VMEM)
    hbm = pl.BlockSpec(memory_space=pl.ANY)
    dma = pltpu.SemaphoreType.DMA
    small = pltpu.VMEM((SIDE, TOK, LANES), BF)
    big = pltpu.VMEM((SIDE, ROWS, WIDE), BF)
    tall = pltpu.VMEM((2, 2, HALF, WIDE), F32)
    halves = pltpu.VMEM((2, 7, HALF, WIDE), BF)
    block = pltpu.VMEM((GROUPS * PAD, WIDE), BF)
    out = jax.ShapeDtypeStruct((TOK, TOK), BF)
    return pl.pallas_call(
        kernel,
        out_shape=(out, out),
        in_specs=[hbm] * 7,
        out_specs=(vm, vm),
        scratch_shapes=[
            pltpu.VMEM((TOK, TOK), BF), pltpu.VMEM((TOK, TOK), BF),
            pltpu.VMEM((2, TOK), jnp.int32), pltpu.VMEM((2, TOK), F32), dma((4,)),
            pltpu.VMEM((SIDE, SIDE, TOK, 2 * HID), BF),
            pltpu.VMEM((HID, SIDE * WIDE), BF),
            pltpu.VMEM((SIDE * LANES, WIDE), BF),
            pltpu.VMEM((ROWS, GROUPS // 2 * PAD), BF),
            block, block, block, block,
            small, small, big, big, tall, tall,
            halves, halves, halves, halves,
            small, small, small, small,
            dma((2 * SIDE + 1,)), dma((2, 8)), dma((2, 8)), dma((8,)), dma((8,)),
            dma((2, 2, 7)), dma((2, 2, 7)), dma((2, 2, 7)), dma((2, 2, 7)),
            dma((8,)), dma((8,)), dma((2, 8)), dma((2, 8)),
        ],
        compiler_params=pltpu.CompilerParams(
            collective_id=0, has_side_effects=True, vmem_limit_bytes=60 * 2**20
        ),
        name="moe",
    )(
        tokens, cotangent, routes.T, route_weight.T,
        w_gate.reshape(SIDE, SIDE, TOK, HID), w_up.reshape(SIDE, SIDE, TOK, HID), w_down[0],
    )


def solution(mesh):
    return jax.shard_map(
        shards,
        mesh=mesh,
        in_specs=(
            P("expert", "tensor"),
            P("expert", "tensor"),
            P("expert", None),
            P("expert", None),
            P("expert", None, "tensor"),
            P("expert", None, "tensor"),
            P("expert", "tensor", None),
        ),
        out_specs=(P("expert", "tensor"), P("expert", "tensor")),
        check_vma=False,
    )
```

```python
import jax
import jax.numpy as jnp
from jax import lax
from jax.experimental import pallas as pl
from jax.experimental.pallas import tpu as pltpu
from jax.sharding import PartitionSpec as P

MESH = pl.DeviceIdType.MESH
BF = jnp.bfloat16
F32 = jnp.float32

GROUPS = 8
SIDE = 8
TOK = 48
CAP = 20
PAD = 48
ROWS = GROUPS * CAP
HALF = ROWS // 2
WIDE = SIDE * TOK
HID = 256
LANES = 128
FAR = (4, 3, 5, 2, 6, 1, 7)
NEAR = (0, 1, 7, 2, 6, 3, 5, 4)


def iota(shape, dim):
    return lax.broadcasted_iota(jnp.int32, shape, dim)


def onehot(cond):
    return jnp.where(cond, 1.0, 0.0).astype(BF)


def mm(a, b):
    return lax.dot_general(a, b, (((1,), (0,)), ((), ())), preferred_element_type=F32)


def mm_tn(a, b):
    return lax.dot_general(a, b, (((0,), (0,)), ((), ())), preferred_element_type=F32)


def mm_nt(a, b):
    return lax.dot_general(a, b, (((1,), (1,)), ((), ())), preferred_element_type=F32)


def half(h):
    return pl.ds(h * HALF, HALF)


def kernel(
    tok_h, cot_h, routes_h, rw_h, wg, wu, wd,
    out_ref,
    tok, cot, routes, rw, isem,
    wgu, wdv, spread, comp, dsend, drecv, rsend, rrecv,
    t1, g1, t2, g2, pm, pg, ms, gs, mr, gr, mp, gp, mq, gq,
    wsem, s1, r1, ds_, dr, s2, r2, s3, r3, rs_, rr, s4, r4,
):
    e = lax.axis_index("expert")
    t = lax.axis_index("tensor")
    y = t // SIDE
    z = t % SIDE

    def at_e(d):
        return ((e + d + GROUPS) % GROUPS, t)

    def at_y(d):
        return (e, ((y + d + SIDE) % SIDE) * SIDE + z)

    def at_z(d):
        return (e, y * SIDE + (z + d + SIDE) % SIDE)

    def send(src, dst, ss, rs, where):
        c = pltpu.make_async_remote_copy(
            src_ref=src, dst_ref=dst, send_sem=ss, recv_sem=rs, device_id=where, device_id_type=MESH
        )
        c.start()
        return c

    first = [
        pltpu.make_async_copy(a, b, isem.at[k])
        for k, (a, b) in enumerate(((tok_h, tok), (cot_h, cot), (routes_h, routes), (rw_h, rw)))
    ]
    for c in first:
        c.start()
    bar = pltpu.get_barrier_semaphore()
    for at in (at_y, at_z, at_e):
        for d in FAR:
            pl.semaphore_signal(bar, inc=1, device_id=at(d), device_id_type=MESH)
    loads = []
    for k in range(SIDE):
        loads.append(pltpu.make_async_copy(wg.at[:, k], wgu.at[k, :, :, pl.ds(0, HID)], wsem.at[k]))
        loads.append(pltpu.make_async_copy(wu.at[:, k], wgu.at[k, :, :, pl.ds(HID, HID)], wsem.at[SIDE + k]))
    loads.append(pltpu.make_async_copy(wd, wdv, wsem.at[2 * SIDE]))

    zero = jnp.zeros((TOK, LANES), BF)
    t1[y] = zero
    g1[z] = zero
    first[0].wait()
    first[1].wait()
    t1[y, :, :TOK] = tok[...]
    g1[z, :, :TOK] = cot[...]
    pl.semaphore_wait(bar, 21)

    copies = []
    for d in FAR:
        copies.append(send(t1.at[y], t1.at[y], s1.at[0, d], r1.at[0, d], at_y(d)))
        copies.append(send(g1.at[z], g1.at[z], s1.at[1, d], r1.at[1, d], at_z(d)))
    for c in loads:
        c.start()

    first[2].wait()
    first[3].wait()
    eye = iota((TOK, TOK), 0) == iota((TOK, TOK), 1)

    def column(row):
        return jnp.sum(jnp.where(eye, row, 0.0), axis=1, keepdims=True)

    ids = routes[...].astype(F32)
    e0, e1 = column(ids[0:1]).astype(jnp.int32), column(ids[1:2]).astype(jnp.int32)
    w0, w1 = column(rw[0:1, :]), column(rw[1:2, :])
    lane = iota((TOK, LANES), 1)
    chosen = onehot((lane == e0) | (lane == e1))
    lower = onehot(iota((TOK, TOK), 1) < iota((TOK, TOK), 0))
    earlier = mm(lower, chosen)
    p0 = jnp.sum(jnp.where(lane == e0, earlier, 0.0), axis=1, keepdims=True).astype(jnp.int32) + e0 * PAD
    p1 = jnp.sum(jnp.where(lane == e1, earlier, 0.0), axis=1, keepdims=True).astype(jnp.int32) + e1 * PAD
    slot = iota((TOK, GROUPS * PAD), 1)
    m0 = onehot(slot == p0)
    m1 = onehot(slot == p1)
    n0 = onehot(slot == p0 + CAP)
    n1 = onehot(slot == p1 + CAP)
    l_ = iota((LANES, WIDE), 0)
    c_ = iota((LANES, WIDE), 1)
    for k in range(SIDE):
        spread[pl.ds(k * LANES, LANES), :] = onehot((c_ - l_ == TOK * k) & (l_ < TOK))
    q_ = iota((HALF, GROUPS // 2 * PAD), 1)
    s_ = iota((HALF, GROUPS // 2 * PAD), 0)
    group = ((q_.astype(F32) + 0.5) * (1.0 / PAD)).astype(jnp.int32)
    place = q_ - group * PAD
    row = group * CAP + place
    comp[pl.ds(0, HALF), :] = onehot((row == s_) & (place < CAP))
    comp[pl.ds(HALF, HALF), :] = onehot((row == s_ + CAP) & (place >= CAP) & (place < 2 * CAP))
    def unpack(ref):
        return mm(jnp.concatenate([ref[k] for k in range(SIDE)], axis=1), spread[...])

    for c in copies[0::2]:
        c.wait_recv()
    tu = unpack(t1).astype(BF)
    for c in copies[1::2]:
        c.wait_recv()
    gu = unpack(g1)
    sent = copies
    left = jnp.concatenate([m0 + m1, n0, n1], axis=0)
    right = jnp.concatenate([tu, (w0 * gu).astype(BF), (w1 * gu).astype(BF)], axis=0)
    dsend[...] = mm_tn(left, right).astype(BF)
    mine = pl.ds(pl.multiple_of(e * PAD, PAD), PAD)

    def there(d):
        return pl.ds(pl.multiple_of(((e + d) % GROUPS) * PAD, PAD), PAD)

    def place_of(d):
        return pl.ds(NEAR.index(d) * PAD, PAD)

    copies = {}
    for o in NEAR[1:]:
        d = GROUPS - o
        copies[o] = send(dsend.at[there(d)], drecv.at[place_of(o)], ds_.at[d], dr.at[d], at_e(d))
    drecv[place_of(0), :] = dsend[mine, :]
    for c in sent:
        c.wait_send()

    def arrive(b):
        for o in NEAR[4 * b : 4 * b + 4]:
            if o:
                copies[o].wait_recv()
        rows = mm(comp[...], drecv[pl.ds(b * 4 * PAD, 4 * PAD), :]).astype(BF)
        t2[0, half(b), :] = rows[:HALF]
        g2[0, half(b), :] = rows[HALF:]

    pairs = ((t2, at_z, 0), (g2, at_y, 1))
    moves = {}

    def go(b, n, src, dst, dist):
        for buf, at, a in pairs:
            moves[a, b, n] = send(
                buf.at[src, half(b)], buf.at[dst, half(b)], s2.at[a, b, n], r2.at[a, b, n], at(dist)
            )

    def arrived(b, *ns):
        for n in ns:
            for a in range(2):
                moves[a, b, n].wait_recv()

    def wcols(k):
        return pl.ds(pl.multiple_of(k * WIDE, LANES), WIDE)

    def wrows(k):
        return wgu[k].reshape(WIDE, 2 * HID)

    acc = [[0.0, 0.0], [0.0, 0.0]]

    def use(b, *ds):
        for d in ds:
            acc[b][0] += mm(t2[d, half(b), :], wrows((z + SIDE - d) % SIDE))
            acc[b][1] += mm_nt(g2[d, half(b), :], wdv[:, wcols((y + SIDE - d) % SIDE)])

    def two(b):
        go(b, 0, 0, 2, 2)
        go(b, 1, 0, 6, -2)

    def one(b):
        go(b, 2, 0, 1, 1)
        go(b, 3, 0, 7, -1)

    def pass_on(b):
        for n in (b, 1 - b):
            arrived(b, n)
            src, step = (2, 1) if n == 0 else (6, -1)
            if n == b:
                go(b, 6, src, 4, 2 * step)
            go(b, 4 + n, src, src + step, step)

    state = [None, None]

    def activate(b):
        gate, up = acc[b][0][:, :HID], acc[b][0][:, HID:]
        grad_h = acc[b][1]
        sig = 1.0 / (1.0 + jnp.exp(-gate))
        swish = gate * sig
        hidden = (swish * up).astype(BF)
        grad_gate = (grad_h * up * sig * (1.0 + gate * (1.0 - sig))).astype(BF)
        grad_up = (grad_h * swish).astype(BF)
        state[b] = (hidden, jnp.concatenate([grad_gate, grad_up], axis=1))

    sums = ((ms, mr, at_y, 0), (gs, gr, at_z, 1))
    hops = {}

    def term(b, d):
        hidden, grads = state[b]
        return mm(hidden, wdv[:, wcols((y + d) % SIDE)]), mm_nt(grads, wrows((z + d) % SIDE))

    def give(b, n, values, dist):
        for (sbuf, rbuf, at, a), value in zip(sums, values):
            sbuf[b, n] = value.astype(BF)
            hops[a, b, n] = send(sbuf.at[b, n], rbuf.at[b, n], s3.at[a, b, n], r3.at[a, b, n], at(dist))

    def taken(b, n):
        values = []
        for _, rbuf, _, a in sums:
            hops[a, b, n].wait_recv()
            values.append(rbuf[b, n].astype(F32))
        return values

    def add(*terms):
        return [sum(vs[1:], vs[0]) for vs in zip(*terms)]

    def start_sums(b):
        give(b, 0, term(b, 4), 2 if b == 0 else -2)
        give(b, 1, term(b, 3), 1)
        give(b, 2, term(b, 5), -1)
        give(b, 3, term(b, 1), 1)
        give(b, 4, term(b, 7), -1)
        for i, d in enumerate((2, 6)):
            pm[b, i], pg[b, i] = term(b, d)

    def kept(b, d):
        return [pm[b, (d - 2) // 4], pg[b, (d - 2) // 4]]

    def middle_sums(b):
        for way in (1 - b, b):
            d, n = ((2, 1), (6, 2))[way]
            parts = [kept(b, d), taken(b, n)]
            if way == b:
                parts.append(taken(b, 0))
            give(b, 5 + way, add(*parts), 2 if way == 0 else -2)

    backs = []

    def end_sums(b):
        total = add(term(b, 0), taken(b, 3), taken(b, 4), taken(b, 5), taken(b, 6))
        both = jnp.concatenate([v.astype(BF) for v in total], axis=0)
        rsend[pl.ds(b * 4 * PAD, 4 * PAD), :] = mm_tn(comp[...], both).astype(BF)
        for o in NEAR[4 * b : 4 * b + 4]:
            if o:
                backs.append(send(rsend.at[place_of(o)], rrecv.at[mine], rs_.at[o], rr.at[o], at_e(o)))
            else:
                rrecv[mine, :] = rsend[place_of(0), :]

    arrive(0)
    two(0)
    one(0)
    arrive(1)
    two(1)
    for c in loads:
        c.wait()
    use(0, 0)
    pass_on(0)
    one(1)
    use(0, 2, 6)
    arrived(0, 2, 3)
    use(0, 1, 7)
    pass_on(1)
    arrived(0, 4, 5, 6)
    use(0, 3, 5, 4)
    activate(0)
    start_sums(0)
    use(1, 0, 2, 6)
    arrived(1, 2, 3)
    use(1, 1, 7)
    middle_sums(0)
    arrived(1, 4, 5, 6)
    use(1, 3, 5, 4)
    activate(1)
    start_sums(1)
    end_sums(0)
    middle_sums(1)
    end_sums(1)
    for c in (*copies.values(), *moves.values(), *hops.values()):
        c.wait_send()
    for c in backs:
        c.wait_recv()
    back = rrecv[...]

    def spread_out(values, buf):
        flat = mm_nt(values, spread[...]).astype(BF)
        for k in range(SIDE):
            buf[k] = flat[:, k * LANES:(k + 1) * LANES]

    spread_out((w0 * mm(m0, back) + w1 * mm(m1, back)).astype(BF), mp)
    last = [send(mp.at[(z + d) % SIDE], mq.at[d], s4.at[0, d], r4.at[0, d], at_z(d)) for d in FAR]
    spread_out(mm(n0 + n1, back).astype(BF), gp)
    last += [send(gp.at[(y + d) % SIDE], gq.at[d], s4.at[1, d], r4.at[1, d], at_y(d)) for d in FAR]
    mtot = mp[z].astype(F32)
    gtot = gp[y].astype(F32)
    for c in (*backs, *last):
        c.wait_send()
    for c in last:
        c.wait_recv()
    for d in range(1, 8):
        mtot += mq[d].astype(F32)
        gtot += gq[d].astype(F32)
    out_ref[0] = mtot[:, :TOK].astype(BF)
    out_ref[1] = gtot[:, :TOK].astype(BF)


def shards(tokens, cotangent, routes, route_weight, w_gate, w_up, w_down):
    vm = pl.BlockSpec(memory_space=pltpu.VMEM)
    hbm = pl.BlockSpec(memory_space=pl.ANY)
    dma = pltpu.SemaphoreType.DMA
    small = pltpu.VMEM((SIDE, TOK, LANES), BF)
    big = pltpu.VMEM((SIDE, ROWS, WIDE), BF)
    tall = pltpu.VMEM((2, 2, HALF, WIDE), F32)
    halves = pltpu.VMEM((2, 7, HALF, WIDE), BF)
    block = pltpu.VMEM((GROUPS * PAD, WIDE), BF)
    both = pl.pallas_call(
        kernel,
        out_shape=jax.ShapeDtypeStruct((2, TOK, TOK), BF),
        in_specs=[hbm] * 7,
        out_specs=vm,
        scratch_shapes=[
            pltpu.VMEM((TOK, TOK), BF), pltpu.VMEM((TOK, TOK), BF),
            pltpu.VMEM((2, TOK), jnp.int32), pltpu.VMEM((2, TOK), F32), dma((4,)),
            pltpu.VMEM((SIDE, SIDE, TOK, 2 * HID), BF),
            pltpu.VMEM((HID, SIDE * WIDE), BF),
            pltpu.VMEM((SIDE * LANES, WIDE), BF),
            pltpu.VMEM((ROWS, GROUPS // 2 * PAD), BF),
            block, block, block, block,
            small, small, big, big, tall, tall,
            halves, halves, halves, halves,
            small, small, small, small,
            dma((2 * SIDE + 1,)), dma((2, 8)), dma((2, 8)), dma((8,)), dma((8,)),
            dma((2, 2, 7)), dma((2, 2, 7)), dma((2, 2, 7)), dma((2, 2, 7)),
            dma((8,)), dma((8,)), dma((2, 8)), dma((2, 8)),
        ],
        compiler_params=pltpu.CompilerParams(
            collective_id=0, has_side_effects=True, vmem_limit_bytes=60 * 2**20
        ),
        name="moe",
    )(
        tokens, cotangent, routes.T, route_weight.T,
        w_gate.reshape(SIDE, SIDE, TOK, HID), w_up.reshape(SIDE, SIDE, TOK, HID), w_down[0],
    )
    return both[0], both[1]


def solution(mesh):
    return jax.shard_map(
        shards,
        mesh=mesh,
        in_specs=(
            P("expert", "tensor"),
            P("expert", "tensor"),
            P("expert", None),
            P("expert", None),
            P("expert", None, "tensor"),
            P("expert", None, "tensor"),
            P("expert", "tensor", None),
        ),
        out_specs=(P("expert", "tensor"), P("expert", "tensor")),
        check_vma=False,
    )
```

```python
import jax
import jax.numpy as jnp
from jax import lax
from jax.experimental import pallas as pl
from jax.experimental.pallas import tpu as pltpu
from jax.sharding import PartitionSpec as P

MESH = pl.DeviceIdType.MESH
BF = jnp.bfloat16
F32 = jnp.float32

GROUPS = 8
SIDE = 8
TOK = 48
CAP = 20
PAD = 48
ROWS = GROUPS * CAP
HALF = ROWS // 2
WIDE = SIDE * TOK
HID = 256
LANES = 128
FAR = (4, 3, 5, 2, 6, 1, 7)
NEAR = (0, 1, 7, 2, 6, 3, 5, 4)


def iota(shape, dim):
    return lax.broadcasted_iota(jnp.int32, shape, dim)


def onehot(cond):
    return jnp.where(cond, 1.0, 0.0).astype(BF)


def mm(a, b):
    return lax.dot_general(a, b, (((1,), (0,)), ((), ())), preferred_element_type=F32)


def mm_tn(a, b):
    return lax.dot_general(a, b, (((0,), (0,)), ((), ())), preferred_element_type=F32)


def mm_nt(a, b):
    return lax.dot_general(a, b, (((1,), (1,)), ((), ())), preferred_element_type=F32)


def half(h):
    return pl.ds(h * HALF, HALF)


def kernel(
    tok_h, cot_h, routes_h, rw_h, wg, wu, wd,
    out_ref,
    tok, cot, routes, rw, isem,
    wgu, wdv, comp, dsend, drecv, rsend, rrecv,
    t1, g1, t2, g2, pm, pg, ms, gs, mr, gr, mp, gp, mq, gq,
    wsem, s1, r1, ds_, dr, s2, r2, s3, r3, rs_, rr, s4, r4,
):
    e = lax.axis_index("expert")
    t = lax.axis_index("tensor")
    y = t // SIDE
    z = t % SIDE

    def at_e(d):
        return ((e + d + GROUPS) % GROUPS, t)

    def at_y(d):
        return (e, ((y + d + SIDE) % SIDE) * SIDE + z)

    def at_z(d):
        return (e, y * SIDE + (z + d + SIDE) % SIDE)

    def send(src, dst, ss, rs, where):
        c = pltpu.make_async_remote_copy(
            src_ref=src, dst_ref=dst, send_sem=ss, recv_sem=rs, device_id=where, device_id_type=MESH
        )
        c.start()
        return c

    first = [
        pltpu.make_async_copy(a, b, isem.at[k])
        for k, (a, b) in enumerate(((tok_h, tok), (cot_h, cot), (routes_h, routes), (rw_h, rw)))
    ]
    for c in first:
        c.start()
    bar = pltpu.get_barrier_semaphore()
    for at in (at_y, at_z, at_e):
        for d in FAR:
            pl.semaphore_signal(bar, inc=1, device_id=at(d), device_id_type=MESH)
    loads = []
    for k in range(SIDE):
        loads.append(pltpu.make_async_copy(wg.at[:, k], wgu.at[k, :, :, pl.ds(0, HID)], wsem.at[k]))
        loads.append(pltpu.make_async_copy(wu.at[:, k], wgu.at[k, :, :, pl.ds(HID, HID)], wsem.at[SIDE + k]))
    loads.append(pltpu.make_async_copy(wd, wdv, wsem.at[2 * SIDE]))

    zero = jnp.zeros((TOK, LANES), BF)
    t1[y] = zero
    g1[z] = zero
    first[0].wait()
    first[1].wait()
    t1[y, :, :TOK] = tok[...]
    g1[z, :, :TOK] = cot[...]
    pl.semaphore_wait(bar, 21)

    copies = []
    for d in FAR:
        copies.append(send(t1.at[y], t1.at[y], s1.at[0, d], r1.at[0, d], at_y(d)))
        copies.append(send(g1.at[z], g1.at[z], s1.at[1, d], r1.at[1, d], at_z(d)))
    for c in loads:
        c.start()

    first[2].wait()
    first[3].wait()
    eye = iota((TOK, TOK), 0) == iota((TOK, TOK), 1)

    def column(row):
        return jnp.sum(jnp.where(eye, row, 0.0), axis=1, keepdims=True)

    ids = routes[...].astype(F32)
    e0, e1 = column(ids[0:1]).astype(jnp.int32), column(ids[1:2]).astype(jnp.int32)
    w0, w1 = column(rw[0:1, :]), column(rw[1:2, :])
    lane = iota((TOK, LANES), 1)
    chosen = onehot((lane == e0) | (lane == e1))
    lower = onehot(iota((TOK, TOK), 1) < iota((TOK, TOK), 0))
    earlier = mm(lower, chosen)
    p0 = jnp.sum(jnp.where(lane == e0, earlier, 0.0), axis=1, keepdims=True).astype(jnp.int32) + e0 * PAD
    p1 = jnp.sum(jnp.where(lane == e1, earlier, 0.0), axis=1, keepdims=True).astype(jnp.int32) + e1 * PAD
    slot = iota((TOK, GROUPS * PAD), 1)
    m0 = onehot(slot == p0)
    m1 = onehot(slot == p1)
    n0 = onehot(slot == p0 + CAP)
    n1 = onehot(slot == p1 + CAP)
    q_ = iota((HALF, GROUPS // 2 * PAD), 1)
    s_ = iota((HALF, GROUPS // 2 * PAD), 0)
    group = ((q_.astype(F32) + 0.5) * (1.0 / PAD)).astype(jnp.int32)
    place = q_ - group * PAD
    row = group * CAP + place
    comp[pl.ds(0, HALF), :] = onehot((row == s_) & (place < CAP))
    comp[pl.ds(HALF, HALF), :] = onehot((row == s_ + CAP) & (place >= CAP) & (place < 2 * CAP))
    starts = [divmod(TOK * k, LANES) for k in range(SIDE)]

    def turn(block, r):
        return pltpu.roll(block, r, 1) if r else block

    def unpack(ref):
        tiles = [0.0] * (WIDE // LANES)
        for k, (j, r) in enumerate(starts):
            block = turn(ref[k].astype(F32), r)
            if r + TOK <= LANES:
                tiles[j] += block
            else:
                tiles[j] += jnp.where(lane >= r, block, 0.0)
                tiles[j + 1] += jnp.where(lane < r + TOK - LANES, block, 0.0)
        return jnp.concatenate(tiles, axis=1)

    for c in copies[0::2]:
        c.wait_recv()
    tu = unpack(t1).astype(BF)
    for c in copies[1::2]:
        c.wait_recv()
    gu = unpack(g1)
    sent = copies
    left = jnp.concatenate([m0 + m1, n0, n1], axis=0)
    right = jnp.concatenate([tu, (w0 * gu).astype(BF), (w1 * gu).astype(BF)], axis=0)
    dsend[...] = mm_tn(left, right).astype(BF)
    mine = pl.ds(pl.multiple_of(e * PAD, PAD), PAD)

    def there(d):
        return pl.ds(pl.multiple_of(((e + d) % GROUPS) * PAD, PAD), PAD)

    def place_of(d):
        return pl.ds(NEAR.index(d) * PAD, PAD)

    copies = {}
    for o in NEAR[1:]:
        d = GROUPS - o
        copies[o] = send(dsend.at[there(d)], drecv.at[place_of(o)], ds_.at[d], dr.at[d], at_e(d))
    drecv[place_of(0), :] = dsend[mine, :]
    for c in sent:
        c.wait_send()

    def arrive(b):
        for o in NEAR[4 * b : 4 * b + 4]:
            if o:
                copies[o].wait_recv()
        rows = mm(comp[...], drecv[pl.ds(b * 4 * PAD, 4 * PAD), :]).astype(BF)
        t2[0, half(b), :] = rows[:HALF]
        g2[0, half(b), :] = rows[HALF:]

    pairs = ((t2, at_z, 0), (g2, at_y, 1))
    moves = {}

    def go(b, n, src, dst, dist):
        for buf, at, a in pairs:
            moves[a, b, n] = send(
                buf.at[src, half(b)], buf.at[dst, half(b)], s2.at[a, b, n], r2.at[a, b, n], at(dist)
            )

    def arrived(b, *ns):
        for n in ns:
            for a in range(2):
                moves[a, b, n].wait_recv()

    def wcols(k):
        return pl.ds(pl.multiple_of(k * WIDE, LANES), WIDE)

    def wrows(k):
        return wgu[k].reshape(WIDE, 2 * HID)

    acc = [[0.0, 0.0], [0.0, 0.0]]

    def use(b, *ds):
        for d in ds:
            acc[b][0] += mm(t2[d, half(b), :], wrows((z + SIDE - d) % SIDE))
            acc[b][1] += mm_nt(g2[d, half(b), :], wdv[:, wcols((y + SIDE - d) % SIDE)])

    def two(b):
        go(b, 0, 0, 2, 2)
        go(b, 1, 0, 6, -2)

    def one(b):
        go(b, 2, 0, 1, 1)
        go(b, 3, 0, 7, -1)

    def pass_on(b):
        for n in (b, 1 - b):
            arrived(b, n)
            src, step = (2, 1) if n == 0 else (6, -1)
            if n == b:
                go(b, 6, src, 4, 2 * step)
            go(b, 4 + n, src, src + step, step)

    state = [None, None]

    def activate(b):
        gate, up = acc[b][0][:, :HID], acc[b][0][:, HID:]
        grad_h = acc[b][1]
        sig = 1.0 / (1.0 + jnp.exp(-gate))
        swish = gate * sig
        hidden = (swish * up).astype(BF)
        grad_gate = (grad_h * up * sig * (1.0 + gate * (1.0 - sig))).astype(BF)
        grad_up = (grad_h * swish).astype(BF)
        state[b] = (hidden, jnp.concatenate([grad_gate, grad_up], axis=1))

    sums = ((ms, mr, at_y, 0), (gs, gr, at_z, 1))
    hops = {}

    def term(b, d):
        hidden, grads = state[b]
        return mm(hidden, wdv[:, wcols((y + d) % SIDE)]), mm_nt(grads, wrows((z + d) % SIDE))

    def give(b, n, values, dist):
        for (sbuf, rbuf, at, a), value in zip(sums, values):
            sbuf[b, n] = value.astype(BF)
            hops[a, b, n] = send(sbuf.at[b, n], rbuf.at[b, n], s3.at[a, b, n], r3.at[a, b, n], at(dist))

    def taken(b, n):
        values = []
        for _, rbuf, _, a in sums:
            hops[a, b, n].wait_recv()
            values.append(rbuf[b, n].astype(F32))
        return values

    def add(*terms):
        return [sum(vs[1:], vs[0]) for vs in zip(*terms)]

    def start_sums(b):
        give(b, 0, term(b, 4), 2 if b == 0 else -2)
        give(b, 1, term(b, 3), 1)
        give(b, 2, term(b, 5), -1)
        give(b, 3, term(b, 1), 1)
        give(b, 4, term(b, 7), -1)
        for i, d in enumerate((2, 6)):
            pm[b, i], pg[b, i] = term(b, d)

    def kept(b, d):
        return [pm[b, (d - 2) // 4], pg[b, (d - 2) // 4]]

    def middle_sums(b):
        for way in (1 - b, b):
            d, n = ((2, 1), (6, 2))[way]
            parts = [kept(b, d), taken(b, n)]
            if way == b:
                parts.append(taken(b, 0))
            give(b, 5 + way, add(*parts), 2 if way == 0 else -2)

    backs = []

    def end_sums(b):
        total = add(term(b, 0), taken(b, 3), taken(b, 4), taken(b, 5), taken(b, 6))
        both = jnp.concatenate([v.astype(BF) for v in total], axis=0)
        rsend[pl.ds(b * 4 * PAD, 4 * PAD), :] = mm_tn(comp[...], both).astype(BF)
        for o in NEAR[4 * b : 4 * b + 4]:
            if o:
                backs.append(send(rsend.at[place_of(o)], rrecv.at[mine], rs_.at[o], rr.at[o], at_e(o)))
            else:
                rrecv[mine, :] = rsend[place_of(0), :]

    arrive(0)
    two(0)
    one(0)
    arrive(1)
    two(1)
    for c in loads:
        c.wait()
    use(0, 0)
    pass_on(0)
    one(1)
    use(0, 2)
    pass_on(1)
    use(0, 6)
    arrived(0, 2, 3)
    use(0, 1, 7)
    arrived(0, 4, 5, 6)
    use(0, 3, 5, 4)
    activate(0)
    start_sums(0)
    use(1, 0, 2, 6)
    arrived(1, 2, 3)
    use(1, 1, 7)
    arrived(1, 4, 5, 6)
    middle_sums(0)
    use(1, 3, 5, 4)
    activate(1)
    start_sums(1)
    end_sums(0)
    middle_sums(1)
    end_sums(1)
    for c in (*copies.values(), *moves.values(), *hops.values()):
        c.wait_send()
    for c in backs:
        c.wait_recv()
    back = rrecv[...]

    def spread_out(values, buf):
        for k, (j, r) in enumerate(starts):
            block = turn(values[:, j * LANES:(j + 1) * LANES], (LANES - r) % LANES)
            if r + TOK > LANES:
                after = turn(values[:, (j + 1) * LANES:(j + 2) * LANES], LANES - r)
                block = jnp.where(lane < LANES - r, block, after)
            buf[k] = block.astype(BF)

    spread_out(w0 * mm(m0, back) + w1 * mm(m1, back), mp)
    last = [send(mp.at[(z + d) % SIDE], mq.at[d], s4.at[0, d], r4.at[0, d], at_z(d)) for d in FAR]
    spread_out(mm(n0 + n1, back), gp)
    last += [send(gp.at[(y + d) % SIDE], gq.at[d], s4.at[1, d], r4.at[1, d], at_y(d)) for d in FAR]
    mtot = mp[z].astype(F32)
    gtot = gp[y].astype(F32)
    for c in (*backs, *last):
        c.wait_send()
    for c in last:
        c.wait_recv()
    for d in range(1, 8):
        mtot += mq[d].astype(F32)
        gtot += gq[d].astype(F32)
    out_ref[0] = mtot[:, :TOK].astype(BF)
    out_ref[1] = gtot[:, :TOK].astype(BF)


def shards(tokens, cotangent, routes, route_weight, w_gate, w_up, w_down):
    vm = pl.BlockSpec(memory_space=pltpu.VMEM)
    hbm = pl.BlockSpec(memory_space=pl.ANY)
    dma = pltpu.SemaphoreType.DMA
    small = pltpu.VMEM((SIDE, TOK, LANES), BF)
    big = pltpu.VMEM((SIDE, ROWS, WIDE), BF)
    tall = pltpu.VMEM((2, 2, HALF, WIDE), F32)
    halves = pltpu.VMEM((2, 7, HALF, WIDE), BF)
    block = pltpu.VMEM((GROUPS * PAD, WIDE), BF)
    both = pl.pallas_call(
        kernel,
        out_shape=jax.ShapeDtypeStruct((2, TOK, TOK), BF),
        in_specs=[hbm] * 7,
        out_specs=vm,
        scratch_shapes=[
            pltpu.VMEM((TOK, TOK), BF), pltpu.VMEM((TOK, TOK), BF),
            pltpu.VMEM((2, TOK), jnp.int32), pltpu.VMEM((2, TOK), F32), dma((4,)),
            pltpu.VMEM((SIDE, SIDE, TOK, 2 * HID), BF),
            pltpu.VMEM((HID, SIDE * WIDE), BF),
            pltpu.VMEM((ROWS, GROUPS // 2 * PAD), BF),
            block, block, block, block,
            small, small, big, big, tall, tall,
            halves, halves, halves, halves,
            small, small, small, small,
            dma((2 * SIDE + 1,)), dma((2, 8)), dma((2, 8)), dma((8,)), dma((8,)),
            dma((2, 2, 7)), dma((2, 2, 7)), dma((2, 2, 7)), dma((2, 2, 7)),
            dma((8,)), dma((8,)), dma((2, 8)), dma((2, 8)),
        ],
        compiler_params=pltpu.CompilerParams(
            collective_id=0, has_side_effects=True, vmem_limit_bytes=60 * 2**20
        ),
        name="moe",
    )(
        tokens, cotangent, routes.T, route_weight.T,
        w_gate.reshape(SIDE, SIDE, TOK, HID), w_up.reshape(SIDE, SIDE, TOK, HID), w_down[0],
    )
    return both[0], both[1]


def solution(mesh):
    return jax.shard_map(
        shards,
        mesh=mesh,
        in_specs=(
            P("expert", "tensor"),
            P("expert", "tensor"),
            P("expert", None),
            P("expert", None),
            P("expert", None, "tensor"),
            P("expert", None, "tensor"),
            P("expert", "tensor", None),
        ),
        out_specs=(P("expert", "tensor"), P("expert", "tensor")),
        check_vma=False,
    )
```

```python
import jax
import jax.numpy as jnp
from jax import lax
from jax.experimental import pallas as pl
from jax.experimental.pallas import tpu as pltpu
from jax.sharding import PartitionSpec as P

MESH = pl.DeviceIdType.MESH
BF = jnp.bfloat16
F32 = jnp.float32

GROUPS = 8
SIDE = 8
TOK = 48
CAP = 20
PAD = 48
ROWS = GROUPS * CAP
HALF = ROWS // 2
WIDE = SIDE * TOK
HID = 256
LANES = 128
FAR = (4, 3, 5, 2, 6, 1, 7)
NEAR = (0, 1, 7, 2, 6, 3, 5, 4)


def iota(shape, dim):
    return lax.broadcasted_iota(jnp.int32, shape, dim)


def onehot(cond):
    return jnp.where(cond, 1.0, 0.0).astype(BF)


def mm(a, b):
    return lax.dot_general(a, b, (((1,), (0,)), ((), ())), preferred_element_type=F32)


def mm_tn(a, b):
    return lax.dot_general(a, b, (((0,), (0,)), ((), ())), preferred_element_type=F32)


def mm_nt(a, b):
    return lax.dot_general(a, b, (((1,), (1,)), ((), ())), preferred_element_type=F32)


def half(h):
    return pl.ds(h * HALF, HALF)


def kernel(
    tok_h, cot_h, routes_h, rw_h, wg, wu, wd,
    out_ref,
    tok, cot, routes, rw, isem,
    wgu, wdv, comp, dsend, drecv, rsend, rrecv,
    t1, g1, t2, g2, pm, pg, ms, gs, mr, gr, mp, gp, mq, gq,
    wsem, s1, r1, ds_, dr, s2, r2, s3, r3, rs_, rr, s4, r4,
):
    e = lax.axis_index("expert")
    t = lax.axis_index("tensor")
    y = t // SIDE
    z = t % SIDE

    def at_e(d):
        return ((e + d + GROUPS) % GROUPS, t)

    def at_y(d):
        return (e, ((y + d + SIDE) % SIDE) * SIDE + z)

    def at_z(d):
        return (e, y * SIDE + (z + d + SIDE) % SIDE)

    def send(src, dst, ss, rs, where):
        c = pltpu.make_async_remote_copy(
            src_ref=src, dst_ref=dst, send_sem=ss, recv_sem=rs, device_id=where, device_id_type=MESH
        )
        c.start()
        return c

    first = [
        pltpu.make_async_copy(a, b, isem.at[k])
        for k, (a, b) in enumerate(((tok_h, tok), (cot_h, cot), (routes_h, routes), (rw_h, rw)))
    ]
    for c in first:
        c.start()
    bar = pltpu.get_barrier_semaphore()
    for at in (at_y, at_z, at_e):
        for d in FAR:
            pl.semaphore_signal(bar, inc=1, device_id=at(d), device_id_type=MESH)
    loads = []
    for k in range(SIDE):
        loads.append(pltpu.make_async_copy(wg.at[:, k], wgu.at[k, :, :, pl.ds(0, HID)], wsem.at[k]))
        loads.append(pltpu.make_async_copy(wu.at[:, k], wgu.at[k, :, :, pl.ds(HID, HID)], wsem.at[SIDE + k]))
    loads.append(pltpu.make_async_copy(wd, wdv, wsem.at[2 * SIDE]))

    zero = jnp.zeros((TOK, LANES), BF)
    t1[y] = zero
    g1[z] = zero
    first[0].wait()
    first[1].wait()
    t1[y, :, :TOK] = tok[...]
    g1[z, :, :TOK] = cot[...]
    pl.semaphore_wait(bar, 21)

    copies = []
    for d in FAR:
        copies.append(send(t1.at[y], t1.at[y], s1.at[0, d], r1.at[0, d], at_y(d)))
        copies.append(send(g1.at[z], g1.at[z], s1.at[1, d], r1.at[1, d], at_z(d)))
    for c in loads:
        c.start()

    first[2].wait()
    first[3].wait()
    eye = iota((TOK, TOK), 0) == iota((TOK, TOK), 1)

    def column(row):
        return jnp.sum(jnp.where(eye, row, 0.0), axis=1, keepdims=True)

    ids = routes[...].astype(F32)
    e0, e1 = column(ids[0:1]).astype(jnp.int32), column(ids[1:2]).astype(jnp.int32)
    w0, w1 = column(rw[0:1, :]), column(rw[1:2, :])
    lane = iota((TOK, LANES), 1)
    chosen = onehot((lane == e0) | (lane == e1))
    lower = onehot(iota((TOK, TOK), 1) < iota((TOK, TOK), 0))
    earlier = mm(lower, chosen)
    p0 = jnp.sum(jnp.where(lane == e0, earlier, 0.0), axis=1, keepdims=True).astype(jnp.int32) + e0 * PAD
    p1 = jnp.sum(jnp.where(lane == e1, earlier, 0.0), axis=1, keepdims=True).astype(jnp.int32) + e1 * PAD
    slot = iota((TOK, GROUPS * PAD), 1)
    m0 = onehot(slot == p0)
    m1 = onehot(slot == p1)
    n0 = onehot(slot == p0 + CAP)
    n1 = onehot(slot == p1 + CAP)
    q_ = iota((HALF, GROUPS // 2 * PAD), 1)
    s_ = iota((HALF, GROUPS // 2 * PAD), 0)
    group = ((q_.astype(F32) + 0.5) * (1.0 / PAD)).astype(jnp.int32)
    place = q_ - group * PAD
    row = group * CAP + place
    comp[pl.ds(0, HALF), :] = onehot((row == s_) & (place < CAP))
    comp[pl.ds(HALF, HALF), :] = onehot((row == s_ + CAP) & (place >= CAP) & (place < 2 * CAP))
    starts = [divmod(TOK * k, LANES) for k in range(SIDE)]

    def turn(block, r):
        return pltpu.roll(block, r, 1) if r else block

    def unpack(ref):
        tiles = [0.0] * (WIDE // LANES)
        for k, (j, r) in enumerate(starts):
            block = turn(ref[k].astype(F32), r)
            if r + TOK <= LANES:
                tiles[j] += block
            else:
                tiles[j] += jnp.where(lane >= r, block, 0.0)
                tiles[j + 1] += jnp.where(lane < r + TOK - LANES, block, 0.0)
        return jnp.concatenate(tiles, axis=1)

    for c in copies[0::2]:
        c.wait_recv()
    tu = unpack(t1).astype(BF)
    for c in copies[1::2]:
        c.wait_recv()
    gu = unpack(g1)
    sent = copies
    left = jnp.concatenate([m0 + m1, n0, n1], axis=0)
    right = jnp.concatenate([tu, (w0 * gu).astype(BF), (w1 * gu).astype(BF)], axis=0)
    dsend[...] = mm_tn(left, right).astype(BF)
    mine = pl.ds(pl.multiple_of(e * PAD, PAD), PAD)

    def there(d):
        return pl.ds(pl.multiple_of(((e + d) % GROUPS) * PAD, PAD), PAD)

    def place_of(d):
        return pl.ds(NEAR.index(d) * PAD, PAD)

    copies = {}
    for o in NEAR[1:]:
        d = GROUPS - o
        copies[o] = send(dsend.at[there(d)], drecv.at[place_of(o)], ds_.at[d], dr.at[d], at_e(d))
    drecv[place_of(0), :] = dsend[mine, :]
    for c in sent:
        c.wait_send()

    def arrive(b):
        for o in NEAR[4 * b : 4 * b + 4]:
            if o:
                copies[o].wait_recv()
        rows = mm(comp[...], drecv[pl.ds(b * 4 * PAD, 4 * PAD), :]).astype(BF)
        t2[0, half(b), :] = rows[:HALF]
        g2[0, half(b), :] = rows[HALF:]

    pairs = ((t2, at_z, 0), (g2, at_y, 1))
    moves = {}

    def go(b, n, src, dst, dist):
        for buf, at, a in pairs:
            moves[a, b, n] = send(
                buf.at[src, half(b)], buf.at[dst, half(b)], s2.at[a, b, n], r2.at[a, b, n], at(dist)
            )

    def arrived(b, *ns):
        for n in ns:
            for a in range(2):
                moves[a, b, n].wait_recv()

    def wcols(k):
        return pl.ds(pl.multiple_of(k * WIDE, LANES), WIDE)

    def wrows(k):
        return wgu[k].reshape(WIDE, 2 * HID)

    acc = [[0.0, 0.0], [0.0, 0.0]]

    def use(b, *ds):
        for d in ds:
            acc[b][0] += mm(t2[d, half(b), :], wrows((z + SIDE - d) % SIDE))
            acc[b][1] += mm_nt(g2[d, half(b), :], wdv[:, wcols((y + SIDE - d) % SIDE)])

    def two(b):
        go(b, 0, 0, 2, 2)
        go(b, 1, 0, 6, -2)

    def one(b):
        go(b, 2, 0, 1, 1)
        go(b, 3, 0, 7, -1)

    def pass_on(b):
        for n in (b, 1 - b):
            arrived(b, n)
            src, step = (2, 1) if n == 0 else (6, -1)
            if n == b:
                go(b, 6, src, 4, 2 * step)
            go(b, 4 + n, src, src + step, step)

    state = [None, None]

    def activate(b):
        gate, up = acc[b][0][:, :HID], acc[b][0][:, HID:]
        grad_h = acc[b][1]
        sig = 1.0 / (1.0 + jnp.exp(-gate))
        swish = gate * sig
        hidden = (swish * up).astype(BF)
        grad_gate = (grad_h * up * sig * (1.0 + gate * (1.0 - sig))).astype(BF)
        grad_up = (grad_h * swish).astype(BF)
        state[b] = (hidden, jnp.concatenate([grad_gate, grad_up], axis=1))

    sums = ((ms, mr, at_y, 0), (gs, gr, at_z, 1))
    hops = {}

    def term(b, d):
        hidden, grads = state[b]
        return mm(hidden, wdv[:, wcols((y + d) % SIDE)]), mm_nt(grads, wrows((z + d) % SIDE))

    def give(b, n, values, dist):
        for (sbuf, rbuf, at, a), value in zip(sums, values):
            sbuf[b, n] = value.astype(BF)
            hops[a, b, n] = send(sbuf.at[b, n], rbuf.at[b, n], s3.at[a, b, n], r3.at[a, b, n], at(dist))

    def taken(b, n):
        values = []
        for _, rbuf, _, a in sums:
            hops[a, b, n].wait_recv()
            values.append(rbuf[b, n].astype(F32))
        return values

    def add(*terms):
        return [sum(vs[1:], vs[0]) for vs in zip(*terms)]

    def start_sums(b):
        give(b, 0, term(b, 4), 2 if b == 0 else -2)
        give(b, 1, term(b, 3), 1)
        give(b, 2, term(b, 5), -1)
        give(b, 3, term(b, 1), 1)
        give(b, 4, term(b, 7), -1)
        for i, d in enumerate((2, 6)):
            pm[b, i], pg[b, i] = term(b, d)

    def kept(b, d):
        return [pm[b, (d - 2) // 4], pg[b, (d - 2) // 4]]

    def middle_sums(b):
        for way in (1 - b, b):
            d, n = ((2, 1), (6, 2))[way]
            parts = [kept(b, d), taken(b, n)]
            if way == b:
                parts.append(taken(b, 0))
            give(b, 5 + way, add(*parts), 2 if way == 0 else -2)

    backs = []

    def end_sums(b):
        total = add(term(b, 0), taken(b, 3), taken(b, 4), taken(b, 5), taken(b, 6))
        both = jnp.concatenate([v.astype(BF) for v in total], axis=0)
        rsend[pl.ds(b * 4 * PAD, 4 * PAD), :] = mm_tn(comp[...], both).astype(BF)
        for o in NEAR[4 * b : 4 * b + 4]:
            if o:
                backs.append(send(rsend.at[place_of(o)], rrecv.at[mine], rs_.at[o], rr.at[o], at_e(o)))
            else:
                rrecv[mine, :] = rsend[place_of(0), :]

    arrive(0)
    two(0)
    one(0)
    arrive(1)
    two(1)
    for c in loads:
        c.wait()
    use(0, 0)
    pass_on(0)
    one(1)
    use(0, 2)
    pass_on(1)
    use(0, 6)
    arrived(0, 2, 3)
    use(0, 1, 7)
    arrived(0, 4, 5, 6)
    use(0, 3, 5, 4)
    activate(0)
    start_sums(0)
    use(1, 0, 2, 6)
    arrived(1, 2, 3)
    use(1, 1, 7)
    arrived(1, 4, 5, 6)
    middle_sums(0)
    use(1, 3, 5, 4)
    activate(1)
    start_sums(1)
    middle_sums(1)
    end_sums(0)
    end_sums(1)
    for c in (*copies.values(), *moves.values(), *hops.values()):
        c.wait_send()
    for c in backs:
        c.wait_recv()
    back = rrecv[...]

    def spread_out(values, buf):
        for k, (j, r) in enumerate(starts):
            block = turn(values[:, j * LANES:(j + 1) * LANES], (LANES - r) % LANES)
            if r + TOK > LANES:
                after = turn(values[:, (j + 1) * LANES:(j + 2) * LANES], LANES - r)
                block = jnp.where(lane < LANES - r, block, after)
            buf[k] = block.astype(BF)

    spread_out(w0 * mm(m0, back) + w1 * mm(m1, back), mp)
    last = [send(mp.at[(z + d) % SIDE], mq.at[d], s4.at[0, d], r4.at[0, d], at_z(d)) for d in FAR]
    spread_out(mm(n0 + n1, back), gp)
    last += [send(gp.at[(y + d) % SIDE], gq.at[d], s4.at[1, d], r4.at[1, d], at_y(d)) for d in FAR]
    mtot = mp[z].astype(F32)
    gtot = gp[y].astype(F32)
    for c in (*backs, *last):
        c.wait_send()
    for c in last:
        c.wait_recv()
    for d in range(1, 8):
        mtot += mq[d].astype(F32)
        gtot += gq[d].astype(F32)
    out_ref[0] = mtot[:, :TOK].astype(BF)
    out_ref[1] = gtot[:, :TOK].astype(BF)


def shards(tokens, cotangent, routes, route_weight, w_gate, w_up, w_down):
    vm = pl.BlockSpec(memory_space=pltpu.VMEM)
    hbm = pl.BlockSpec(memory_space=pl.ANY)
    dma = pltpu.SemaphoreType.DMA
    small = pltpu.VMEM((SIDE, TOK, LANES), BF)
    big = pltpu.VMEM((SIDE, ROWS, WIDE), BF)
    tall = pltpu.VMEM((2, 2, HALF, WIDE), F32)
    halves = pltpu.VMEM((2, 7, HALF, WIDE), BF)
    block = pltpu.VMEM((GROUPS * PAD, WIDE), BF)
    both = pl.pallas_call(
        kernel,
        out_shape=jax.ShapeDtypeStruct((2, TOK, TOK), BF),
        in_specs=[hbm] * 7,
        out_specs=vm,
        scratch_shapes=[
            pltpu.VMEM((TOK, TOK), BF), pltpu.VMEM((TOK, TOK), BF),
            pltpu.VMEM((2, TOK), jnp.int32), pltpu.VMEM((2, TOK), F32), dma((4,)),
            pltpu.VMEM((SIDE, SIDE, TOK, 2 * HID), BF),
            pltpu.VMEM((HID, SIDE * WIDE), BF),
            pltpu.VMEM((ROWS, GROUPS // 2 * PAD), BF),
            block, block, block, block,
            small, small, big, big, tall, tall,
            halves, halves, halves, halves,
            small, small, small, small,
            dma((2 * SIDE + 1,)), dma((2, 8)), dma((2, 8)), dma((8,)), dma((8,)),
            dma((2, 2, 7)), dma((2, 2, 7)), dma((2, 2, 7)), dma((2, 2, 7)),
            dma((8,)), dma((8,)), dma((2, 8)), dma((2, 8)),
        ],
        compiler_params=pltpu.CompilerParams(
            collective_id=0, has_side_effects=True, vmem_limit_bytes=60 * 2**20
        ),
        name="moe",
    )(
        tokens, cotangent, routes.T, route_weight.T,
        w_gate.reshape(SIDE, SIDE, TOK, HID), w_up.reshape(SIDE, SIDE, TOK, HID), w_down[0],
    )
    return both[0], both[1]


def solution(mesh):
    return jax.shard_map(
        shards,
        mesh=mesh,
        in_specs=(
            P("expert", "tensor"),
            P("expert", "tensor"),
            P("expert", None),
            P("expert", None),
            P("expert", None, "tensor"),
            P("expert", None, "tensor"),
            P("expert", "tensor", None),
        ),
        out_specs=(P("expert", "tensor"), P("expert", "tensor")),
        check_vma=False,
    )
```
